256 devices in a mesh: gx: 8 (over z), gy: 4 (over x_lo, core), gz: 8 (over y, x_hi).
Axes of the slice: x: 4 (x_hi: 2, x_lo: 2; x = x_hi * 2 + x_lo), y: 4, z: 8, core: 2. Of those that a mesh axis runs over, the one named last changes fastest.
Arguments:
- tokens: bfloat16 [2048, 6144], P(('gy', 'gx'), 'gz'), may hold values from -6 to 6
- w_in: bfloat16 [6144, 24576], P('gz', ('gx', 'gy')), may hold values from -0.078125 to 0.078125
- w_out: bfloat16 [24576, 6144], P(('gx', 'gy'), 'gz')
- out_grad: bfloat16 [2048, 6144], P(('gy', 'gx'), 'gz')
Outputs:
- in_grad: bfloat16 [2048, 6144], P(('gy', 'gx'), 'gz')
- grad_in_clipped: bfloat16 [6144, 24576], P('gz', ('gx', 'gy'))
- grad_out_clipped: bfloat16 [24576, 6144], P(('gx', 'gy'), 'gz')
The draws below stay inside these ranges and needn't reach their ends.
All inputs are finite; a program needn't handle non-finite values.
Results may differ from the reference program's by a relative error of at most 0.025.
Values may be sent and summed in bfloat16 or wider, within the bound.
A program may use at most 128 MiB of HBM per device.

```python
import math
import jax
import jax.numpy as jnp
from jax import lax

D = 6144
FW = 24576
TOKENS = 2048
N_GZ = 8


def rising_scales(key, count):
    uniform_part = jax.random.uniform(key, (count,), jnp.float32)
    position = jnp.arange(count, dtype=jnp.float32) / count
    return jnp.exp(math.log(3.0) * position + math.log(10.0 / 3.0) * uniform_part)


def draw_w_out(key, part):
    key = jax.random.fold_in(key, 11)
    key_one, key_two = jax.random.split(key)
    row_scale = rising_scales(key_two, FW)
    base = jnp.clip(jax.random.normal(key_one, (FW, D), jnp.float32), -6.0, 6.0)
    return (base * row_scale[:, None] / (4.0 * math.sqrt(FW))).astype(jnp.bfloat16)


def draw_out_grad(key, part):
    key = jax.random.fold_in(key, 23)
    key_one, key_two, key_three = jax.random.split(key, 3)
    col_scale = rising_scales(key_two, D)
    row_scale = jnp.exp(math.log(10.0) * jax.random.uniform(key_three, (TOKENS,), jnp.float32))
    base = jnp.clip(jax.random.normal(key_one, (TOKENS, D), jnp.float32), -6.0, 6.0)
    return (base * col_scale[None, :] * row_scale[:, None] / 10.0).astype(jnp.bfloat16)


def block_levels(stream_key, shape, pieces, smallest, largest):
    factor_of, own = 1.0, jax.random.fold_in(stream_key, 6)
    for axis_at, blocks in pieces:
        heights = jnp.exp(jax.random.uniform(jax.random.fold_in(own, axis_at), (blocks,), jnp.float32, smallest / len(pieces), largest / len(pieces)))
        factor_of = factor_of * jnp.repeat(heights, shape[axis_at] // blocks).reshape([-1 if axis == axis_at else 1 for axis in range(len(shape))])
    return factor_of


def bell_draw(stream_key, extent, width, reach, cuts=(), held_as=jnp.bfloat16):
    drawn = width * jax.random.normal(stream_key, extent, jnp.float32)
    if cuts:
        drawn = drawn * block_levels(stream_key, extent, cuts, -0.22, 0.18)
    return jnp.clip(drawn, -reach, reach).astype(held_as)


def setup_inputs(seed: int = 0) -> dict:
    key_of = jax.random.split(jax.random.key(seed), 5)
    tokens = bell_draw(key_of[0], (TOKENS, D), 1.0, 6.0, ((0, 32), (1, 8)))
    w_in = bell_draw(key_of[1], (D, FW), D ** -0.5, 0.078125, ((0, 8), (1, 32)))
    w_out = draw_w_out(jax.random.fold_in(key_of[4], 71), 0)
    out_grad = draw_out_grad(jax.random.fold_in(key_of[4], 71), 0)
    return dict(tokens=tokens, w_in=w_in, w_out=w_out, out_grad=out_grad)


GELU_C = 0.7978845608

def gelu_parts(values):
    inner_arg = GELU_C * (values + 0.044715 * values * values * values)
    tanh_val = jnp.tanh(inner_arg)
    value_out = 0.5 * values * (1.0 + tanh_val)
    slope = 0.5 * (1.0 + tanh_val) + 0.5 * values * (1.0 - tanh_val * tanh_val) * GELU_C * (1.0 + 3.0 * 0.044715 * values * values)
    return (value_out, slope)

def reference(tokens, w_in, w_out, out_grad):
    width_blk = D // N_GZ

    def add_block(running, block_id):
        start = (block_id * width_blk).astype(jnp.int32)
        x_part = lax.dynamic_slice_in_dim(tokens, start, width_blk, 1)
        w_part = lax.dynamic_slice_in_dim(w_in, start, width_blk, 0)
        dy_part = lax.dynamic_slice_in_dim(out_grad, start, width_blk, 1)
        o_part = lax.dynamic_slice_in_dim(w_out, start, width_blk, 1)
        h_term = jnp.dot(x_part, w_part, preferred_element_type=jnp.float32)
        d_term = lax.dot_general(dy_part, o_part, (((1,), (1,)), ((), ())), preferred_element_type=jnp.float32)
        h_term = lax.optimization_barrier(h_term.astype(jnp.bfloat16)).astype(jnp.float32)
        d_term = lax.optimization_barrier(d_term.astype(jnp.bfloat16)).astype(jnp.float32)
        return ((running[0] + h_term, running[1] + d_term), None)
    zeros_init = jnp.zeros((TOKENS, FW), jnp.float32)
    (pre_act, d_act), _ = lax.scan(add_block, (zeros_init, zeros_init), jnp.arange(N_GZ, dtype=jnp.int32))
    value_out, slope = gelu_parts(pre_act)
    act_rows = value_out.astype(jnp.bfloat16)
    d_pre = (d_act * slope).astype(jnp.bfloat16)
    in_grad = lax.dot_general(d_pre, w_in, (((1,), (1,)), ((), ())), preferred_element_type=jnp.float32).astype(jnp.bfloat16)
    grad_in = lax.dot_general(tokens, d_pre, (((0,), (0,)), ((), ())), preferred_element_type=jnp.float32)
    grad_out = lax.dot_general(act_rows, out_grad, (((0,), (0,)), ((), ())), preferred_element_type=jnp.float32)
    square_sum = jnp.sum(grad_in * grad_in) + jnp.sum(grad_out * grad_out)
    factor = 1.0 / jnp.sqrt(square_sum / (2.0 * D * FW) + 1e-06)
    return (in_grad, (grad_in * factor).astype(jnp.bfloat16), (grad_out * factor).astype(jnp.bfloat16))
```

```python
import jax
import jax.numpy as jnp
from jax import lax
from jax.experimental import pallas as pl
from jax.experimental.pallas import tpu as pltpu
from jax.sharding import PartitionSpec as P

D = 6144
FW = 24576
GELU_C = 0.7978845608
MESH = pl.DeviceIdType.MESH

NB = 8
ROWS = 128
HALF = 64
W = 768
Q = 384
F32 = jnp.float32
BF16 = jnp.bfloat16


def gelu_parts(values):
    square = values * values
    inner_arg = GELU_C * (values + 0.044715 * square * values)
    tanh_val = jnp.tanh(inner_arg)
    value_out = 0.5 * values * (1.0 + tanh_val)
    slope = 0.5 * (1.0 + tanh_val) + 0.5 * values * (1.0 - tanh_val * tanh_val) * GELU_C * (
        1.0 + 3.0 * 0.044715 * square
    )
    return (value_out, slope)


def contract(left, right, left_dim, right_dim):
    return lax.dot_general(
        left, right, (((left_dim,), (right_dim,)), ((), ())), preferred_element_type=F32
    )


def kernel(
    tok, win, wout, dy, o_dx, o_gin, o_gout,
    xall, wsib, part, got, xgot, full, acc_in, acc_out, dxs, dxr, gs_in, gs_out, gr_in, gr_out,
    sq, sqr1, sqr2,
    ss, rs, wss, wrs, gss, grs, s1s, s1r, s2s, s2r,
):
    z, gy, gz = lax.axis_index("gx"), lax.axis_index("gy"), lax.axis_index("gz")
    yy, xh = gz // 2, gz % 2
    xl, core = gy // 2, gy % 2
    up, down, far = (yy + 1) % 4, (yy + 3) % 4, (yy + 2) % 4
    to_up, to_down = {"gz": up * 2 + xh}, {"gz": down * 2 + xh}
    to_hi = {"gz": yy * 2 + 1 - xh}
    other_gy = (1 - xl) * 2 + core
    to_lo = {"gy": other_gy}
    to_sib = {"gy": xl * 2 + 1 - core}

    group_one = [
        (dz * 2 + k, {"gx": (z + dz) % 8, "gy": other_gy if k else gy})
        for dz in range(8) for k in range(2) if dz + k
    ]
    group_two = [
        (d * 4 + kx * 2 + kc, {
            "gz": ((yy + d) % 4) * 2 + (1 - xh if kx else xh),
            "gy": xl * 2 + (1 - core if kc else core),
        })
        for d in range(4) for kx in range(2) for kc in range(2) if d + kx + kc
    ]

    def put(src, dst, send, recv, where):
        pltpu.make_async_remote_copy(
            src_ref=src, dst_ref=dst, send_sem=send, recv_sem=recv,
            device_id=where, device_id_type=MESH,
        ).start()

    def arrived(ref, sem):
        pltpu.make_async_remote_copy(
            src_ref=ref, dst_ref=ref, send_sem=sem, recv_sem=sem,
            device_id=to_up, device_id_type=MESH,
        ).wait_recv()

    def left(ref, sem):
        pltpu.make_async_remote_copy(
            src_ref=ref, dst_ref=ref, send_sem=sem, recv_sem=sem,
            device_id=to_up, device_id_type=MESH,
        ).wait_send()

    barrier = pltpu.get_barrier_semaphore()
    for _, where in group_one + group_two:
        pl.semaphore_signal(barrier, inc=1, device_id=where, device_id_type=MESH)
    pl.semaphore_wait(barrier, 30)

    xall[0, 0, 0:HALF] = tok[...]
    xall[0, 1, 0:HALF] = dy[...]
    put(xall.at[0, :, 0:HALF], xall.at[0, :, HALF:ROWS], ss.at[0, 13], rs.at[0, 13], to_lo)
    put(win, wsib.at[0], wss.at[0], wrs.at[0], to_sib)
    put(wout, wsib.at[1], wss.at[1], wrs.at[1], to_sib)

    acc_in[...] = jnp.zeros_like(acc_in)
    acc_out[...] = jnp.zeros_like(acc_out)

    def products(b):
        @pl.when(b == 0)
        def _():
            arrived(xall.at[0, :, HALF:ROWS], rs.at[0, 13])
            put(xall.at[0], xall.at[1], ss.at[1, 13], rs.at[1, 13], {"gx": (z + 1) % 8})
            put(xall.at[0], xall.at[2], ss.at[2, 13], rs.at[2, 13], {"gx": (z + 7) % 8})

        @pl.when(b > 0)
        def _():
            arrived(xall.at[b], rs.at[b, 13])

        @pl.when((b > 0) & (b < NB - 2))
        def _():
            nxt = (z + 7 + 2 * (b % 2)) % 8
            put(xall.at[b], xall.at[b + 2], ss.at[b + 2, 13], rs.at[b + 2, 13], {"gx": nxt})

        def one(which, w_in, w_out):
            h = contract(xall[b, 0], w_in, 1, 0).astype(BF16)
            part[b, 2 * which, 0] = h[:, :Q]
            part[b, 2 * which + 1, 0] = h[:, Q:]
            d = contract(xall[b, 1], w_out, 1, 1).astype(BF16)
            part[b, 2 * which, 1] = d[:, :Q]
            part[b, 2 * which + 1, 1] = d[:, Q:]

        one(0, win[...], wout[...])

        @pl.when(b == 0)
        def _():
            arrived(wsib.at[0], wrs.at[0])
            arrived(wsib.at[1], wrs.at[1])

        one(1, wsib[0], wsib[1])
        put(part.at[b, far, 0], got.at[b, 0], ss.at[b, 0], rs.at[b, 0], to_up)
        put(part.at[b, far, 1], got.at[b, 2], ss.at[b, 2], rs.at[b, 2], to_down)
        put(part.at[b, up, 1], got.at[b, 1], ss.at[b, 1], rs.at[b, 1], to_up)
        put(part.at[b, down, 0], got.at[b, 3], ss.at[b, 3], rs.at[b, 3], to_down)

    def relay_sums(b):
        arrived(got.at[b, 0], rs.at[b, 0])
        part[b, up, 0] = (part[b, up, 0].astype(F32) + got[b, 0].astype(F32)).astype(BF16)
        put(part.at[b, up, 0], got.at[b, 4], ss.at[b, 4], rs.at[b, 4], to_up)
        arrived(got.at[b, 2], rs.at[b, 2])
        part[b, down, 1] = (part[b, down, 1].astype(F32) + got[b, 2].astype(F32)).astype(BF16)
        put(part.at[b, down, 1], got.at[b, 5], ss.at[b, 5], rs.at[b, 5], to_down)

    def quarter_sums(b):
        for k in (1, 3, 4, 5):
            arrived(got.at[b, k], rs.at[b, k])
        part[b, yy, 0] = (
            part[b, yy, 0].astype(F32) + got[b, 3].astype(F32) + got[b, 4].astype(F32)
        ).astype(BF16)
        part[b, yy, 1] = (
            part[b, yy, 1].astype(F32) + got[b, 1].astype(F32) + got[b, 5].astype(F32)
        ).astype(BF16)
        put(part.at[b, yy], xgot.at[b], ss.at[b, 6], rs.at[b, 6], to_hi)

    def activate(b):
        arrived(xgot.at[b], rs.at[b, 6])
        value_out, slope = gelu_parts(part[b, yy, 0].astype(F32) + xgot[b, 0].astype(F32))
        full[b, yy, 0] = value_out.astype(BF16)
        full[b, yy, 1] = (
            (part[b, yy, 1].astype(F32) + xgot[b, 1].astype(F32)) * slope
        ).astype(BF16)
        put(full.at[b, yy], full.at[b, yy], ss.at[b, 7], rs.at[b, 7], to_up)
        put(full.at[b, yy], full.at[b, yy], ss.at[b, 8], rs.at[b, 8], to_down)

    def relay_acts(b):
        arrived(full.at[b, down], rs.at[b, 7])
        put(full.at[b, down, 0], full.at[b, down, 0], ss.at[b, 9], rs.at[b, 9], to_up)
        arrived(full.at[b, up], rs.at[b, 8])
        put(full.at[b, up, 1], full.at[b, up, 1], ss.at[b, 10], rs.at[b, 10], to_down)

    def input_grad(b):
        arrived(full.at[b, far, 0], rs.at[b, 9])
        arrived(full.at[b, far, 1], rs.at[b, 10])
        own = jnp.concatenate([full[b, 0, 1], full[b, 1, 1]], axis=1)
        sib = jnp.concatenate([full[b, 2, 1], full[b, 3, 1]], axis=1)
        dxs[b] = (contract(own, win[...], 1, 1) + contract(sib, wsib[0], 1, 1)).astype(BF16)
        owner = (z + 8 + (b // 2) * (1 - b % 2) - ((b + 1) // 2) * (b % 2)) % 8

        @pl.when(b > 0)
        def _():
            put(dxs.at[b, 0:HALF], dxr.at[b, 0], ss.at[b, 11], rs.at[b, 11], {"gx": owner})

        put(
            dxs.at[b, HALF:ROWS], dxr.at[b, 1], ss.at[b, 12], rs.at[b, 12],
            {"gx": owner, "gy": other_gy},
        )

    def weight_grads(b):
        first = b - 1
        x_t = jnp.concatenate([xall[first, 0], xall[b, 0]], axis=0).T
        dy_pair = jnp.concatenate([xall[first, 1], xall[b, 1]], axis=0)

        @pl.loop(0, 4)
        def _(q):
            act_t = jnp.concatenate([full[first, q, 0], full[b, q, 0]], axis=0).T
            d_pre = jnp.concatenate([full[first, q, 1], full[b, q, 1]], axis=0)
            acc_in[q] += contract(x_t, d_pre, 1, 0)
            acc_out[q] += contract(act_t, dy_pair, 1, 0)

    stages = (products, relay_sums, quarter_sums, activate, relay_acts, input_grad)

    @pl.loop(0, NB + len(stages) - 1)
    def _(t):
        for lag, stage in enumerate(stages):
            b = t - lag

            @pl.when((b >= 0) & (b < NB))
            def _(stage=stage, b=b):
                stage(b)

        last = t - (len(stages) - 1)

        @pl.when((last >= 0) & (last % 2 == 1))
        def _():
            weight_grads(last)

    for j in range(2):
        gs_in[j] = acc_in[2 + j].astype(BF16)
        put(gs_in.at[j], gr_in.at[j], gss.at[j], grs.at[j], to_sib)
        gs_out[j] = acc_out[2 + j].astype(BF16)
        put(gs_out.at[j], gr_out.at[j], gss.at[2 + j], grs.at[2 + j], to_sib)

    total = dxs[0, 0:HALF].astype(F32)
    for b in range(NB):
        for k in range(2):
            if b + k:
                arrived(dxr.at[b, k], rs.at[b, 11 + k])
                total += dxr[b, k].astype(F32)
    o_dx[...] = total.astype(BF16)

    def folded(values):
        rows = jnp.sum((values * values).reshape(-1, 8, values.shape[1]), axis=0)
        out = rows[:, 0:128]
        for i in range(1, values.shape[1] // 128):
            out += rows[:, 128 * i : 128 * (i + 1)]
        return out

    sq[0] = jnp.zeros((8, 128), F32)
    for j in range(2):
        arrived(gr_in.at[j], grs.at[j])
        summed = acc_in[j] + gr_in[j].astype(F32)
        acc_in[j] = summed
        sq[0] += folded(summed)
        arrived(gr_out.at[j], grs.at[2 + j])
        summed = acc_out[j] + gr_out[j].astype(F32)
        acc_out[j] = summed
        sq[0] += folded(summed)

    for slot, where in group_one:
        put(sq.at[0], sqr1.at[slot], s1s.at[slot], s1r.at[slot], where)
    whole = sq[0]
    for slot, _ in group_one:
        arrived(sqr1.at[slot], s1r.at[slot])
        whole += sqr1[slot]
    sq[1] = whole
    for slot, where in group_two:
        put(sq.at[1], sqr2.at[slot], s2s.at[slot], s2r.at[slot], where)
    for slot, _ in group_two:
        arrived(sqr2.at[slot], s2r.at[slot])
        whole += sqr2[slot]
    factor = lax.rsqrt(jnp.sum(whole, keepdims=True) / (2.0 * D * FW) + 1e-06)
    for j in range(2):
        o_gin[:, j * Q : (j + 1) * Q] = (acc_in[j] * factor).astype(BF16)
        o_gout[j * Q : (j + 1) * Q, :] = (acc_out[j] * factor).astype(BF16)

    @pl.loop(0, NB)
    def _(b):
        for k in (0, 1, 2, 3, 4, 5, 9, 10):
            left(got.at[0, 0], ss.at[b, k])
        for k in (6, 7, 8):
            left(full.at[0, 0], ss.at[b, k])

        @pl.when(b > 0)
        def _():
            left(dxs.at[0, 0:HALF], ss.at[b, 11])
            left(xall.at[0], ss.at[b, 13])

        left(dxs.at[0, 0:HALF], ss.at[b, 12])

    left(xall.at[0, :, 0:HALF], ss.at[0, 13])
    for j in range(2):
        left(wsib.at[j], wss.at[j])
        left(gs_in.at[j], gss.at[j])
        left(gs_out.at[j], gss.at[2 + j])
    for slot, _ in group_one:
        left(sq.at[0], s1s.at[slot])
    for slot, _ in group_two:
        left(sq.at[1], s2s.at[slot])


def shards(tokens, w_in, w_out, out_grad):
    vmem = pl.BlockSpec(memory_space=pltpu.VMEM)
    dma = pltpu.SemaphoreType.DMA
    return pl.pallas_call(
        kernel,
        out_shape=(
            jax.ShapeDtypeStruct((HALF, W), BF16),
            jax.ShapeDtypeStruct((W, W), BF16),
            jax.ShapeDtypeStruct((W, W), BF16),
        ),
        in_specs=[vmem] * 4,
        out_specs=(vmem,) * 3,
        scratch_shapes=[
            pltpu.VMEM((NB, 2, ROWS, W), BF16),
            pltpu.VMEM((2, W, W), BF16),
            pltpu.VMEM((NB, 4, 2, ROWS, Q), BF16),
            pltpu.VMEM((NB, 6, ROWS, Q), BF16),
            pltpu.VMEM((NB, 2, ROWS, Q), BF16),
            pltpu.VMEM((NB, 4, 2, ROWS, Q), BF16),
            pltpu.VMEM((4, W, Q), F32),
            pltpu.VMEM((4, Q, W), F32),
            pltpu.VMEM((NB, ROWS, W), BF16),
            pltpu.VMEM((NB, 2, HALF, W), BF16),
            pltpu.VMEM((2, W, Q), BF16),
            pltpu.VMEM((2, Q, W), BF16),
            pltpu.VMEM((2, W, Q), BF16),
            pltpu.VMEM((2, Q, W), BF16),
            pltpu.VMEM((2, 8, 128), F32),
            pltpu.VMEM((16, 8, 128), F32),
            pltpu.VMEM((16, 8, 128), F32),
            dma((NB, 14)), dma((NB, 14)),
            dma((2,)), dma((2,)),
            dma((4,)), dma((4,)),
            dma((16,)), dma((16,)),
            dma((16,)), dma((16,)),
        ],
        compiler_params=pltpu.CompilerParams(
            collective_id=0, has_side_effects=True, vmem_limit_bytes=60 * 2**20
        ),
        cost_estimate=pl.CostEstimate(
            flops=12_100_000_000, bytes_accessed=10_000_000, transcendentals=400_000
        ),
    )(tokens, w_in, w_out, out_grad)


def solution(mesh):
    placed = (
        P(("gy", "gx"), "gz"),
        P("gz", ("gx", "gy")),
        P(("gx", "gy"), "gz"),
        P(("gy", "gx"), "gz"),
    )
    return jax.shard_map(
        shards,
        mesh=mesh,
        in_specs=placed,
        out_specs=(P(("gy", "gx"), "gz"), P("gz", ("gx", "gy")), P(("gx", "gy"), "gz")),
        check_vma=False,
    )
```

```python
import jax
import jax.numpy as jnp
from jax import lax
from jax.experimental import pallas as pl
from jax.experimental.pallas import tpu as pltpu
from jax.sharding import PartitionSpec as P

D = 6144
FW = 24576
GELU_C = 0.7978845608
MESH = pl.DeviceIdType.MESH

NB = 8
ROWS = 128
HALF = 64
W = 768
SPLIT = 4
Q = 384
F32 = jnp.float32
BF16 = jnp.bfloat16


def gelu_parts(values):
    square = values * values
    inner_arg = GELU_C * (values + 0.044715 * square * values)
    tanh_val = jnp.tanh(inner_arg)
    value_out = 0.5 * values * (1.0 + tanh_val)
    slope = 0.5 * (1.0 + tanh_val) + 0.5 * values * (1.0 - tanh_val * tanh_val) * GELU_C * (
        1.0 + 3.0 * 0.044715 * square
    )
    return (value_out, slope)


def contract(left, right, left_dim, right_dim):
    return lax.dot_general(
        left, right, (((left_dim,), (right_dim,)), ((), ())), preferred_element_type=F32
    )


def kernel(
    tok, win, wout, dy, o_dx, o_gin, o_gout, o_sum,
    xall, xsib, wown, wsib, part, got, xgot, full, fsib, acc_in, acc_out, dxs, dxr,
    sq, sqr1, sqr2,
    ls, ss, xr, rs, wrs, srs, crs,
):
    z, gy, gz = lax.axis_index("gx"), lax.axis_index("gy"), lax.axis_index("gz")
    yy, xh = gz // 2, gz % 2
    xl, core = gy // 2, gy % 2
    up, down, far = (yy + 1) % 4, (yy + 3) % 4, (yy + 2) % 4
    to_up, to_down = {"gz": up * 2 + xh}, {"gz": down * 2 + xh}
    hi_gz = yy * 2 + 1 - xh
    other_gy = (1 - xl) * 2 + core
    sib_gy = xl * 2 + 1 - core
    to_hi, to_lo, to_sib = {"gz": hi_gz}, {"gy": other_gy}, {"gy": sib_gy}
    z_up, z_down = {"gx": (z + 1) % 8}, {"gx": (z + 7) % 8}

    group_one = [
        (dz * 2 + k, {"gx": (z + dz) % 8, "gy": other_gy if k else gy})
        for dz in range(8) for k in range(2) if dz + k
    ]
    group_two = [
        (d * 4 + kx * 2 + kc, {
            "gz": ((yy + d) % 4) * 2 + (1 - xh if kx else xh),
            "gy": sib_gy if kc else gy,
        })
        for d in range(4) for kx in range(2) for kc in range(2) if d + kx + kc
    ]
    s_sum, s_act, s_pass, s_move, s_core, s_one, s_two, s_half = [ss.at[i] for i in range(8)]

    def put(src, dst, send, recv, where):
        pltpu.make_async_remote_copy(
            src_ref=src, dst_ref=dst, send_sem=send, recv_sem=recv,
            device_id=where, device_id_type=MESH,
        ).start()

    def arrived(ref, sem):
        pltpu.make_async_remote_copy(
            src_ref=ref, dst_ref=ref, send_sem=sem, recv_sem=sem,
            device_id=to_up, device_id_type=MESH,
        ).wait_recv()

    def left(ref, sem):
        pltpu.make_async_remote_copy(
            src_ref=ref, dst_ref=ref, send_sem=sem, recv_sem=sem,
            device_id=to_up, device_id_type=MESH,
        ).wait_send()

    loads = [
        pltpu.make_async_copy(tok, xall.at[0, 0, 0], ls.at[0]),
        pltpu.make_async_copy(dy, xall.at[0, 0, 1], ls.at[1]),
        pltpu.make_async_copy(win, wown.at[0], ls.at[2]),
        pltpu.make_async_copy(wout, wown.at[1], ls.at[3]),
    ]
    for load in loads:
        load.start()
    barrier = pltpu.get_barrier_semaphore()
    for _, where in group_one + group_two:
        pl.semaphore_signal(barrier, inc=1, device_id=where, device_id_type=MESH)
    acc_in[...] = jnp.zeros_like(acc_in)
    acc_out[...] = jnp.zeros_like(acc_out)
    loads[0].wait()
    loads[1].wait()
    pl.semaphore_wait(barrier, 30)

    put(xall.at[0, 0], xall.at[0, 1], s_move, xr.at[0, 1], to_lo)
    put(xall.at[0, 0], xall.at[1, 0], s_move, xr.at[1, 0], z_up)
    put(xall.at[0, 0], xall.at[1, 1], s_move, xr.at[1, 1], z_down)
    loads[2].wait()
    loads[3].wait()
    put(wown.at[0], wsib.at[0], s_core, wrs.at[0], to_sib)
    put(wown.at[1], wsib.at[1], s_core, wrs.at[1], to_sib)

    def one(b, rows, x, g, which, w_in, w_out):
        h = contract(x, w_in, 1, 0).astype(BF16)
        part[b, 2 * which, 0, rows] = h[:, :Q]
        part[b, 2 * which + 1, 0, rows] = h[:, Q:]
        d = contract(g, w_out, 1, 1).astype(BF16)
        part[b, 2 * which, 1, rows] = d[:, :Q]
        part[b, 2 * which + 1, 1, rows] = d[:, Q:]

    def send_products(b, rows):
        put(part.at[b, far, 0, rows], got.at[6 * b, rows], s_sum, rs.at[b, 0], to_up)
        put(part.at[b, far, 1, rows], got.at[6 * b + 1, rows], s_sum, rs.at[b, 0], to_down)
        put(part.at[b, up, 1, rows], got.at[6 * b + 2, rows], s_sum, rs.at[b, 1], to_up)
        put(part.at[b, down, 0, rows], got.at[6 * b + 3, rows], s_sum, rs.at[b, 1], to_down)

    put(xall.at[0, 0], xsib.at[0, 0], s_half, rs.at[0, 6], to_sib)
    low, high, every = slice(0, HALF), slice(HALF, ROWS), slice(0, ROWS)
    one(0, low, xall[0, 0, 0], xall[0, 0, 1], 0, wown[0], wown[1])
    arrived(wsib.at[0], wrs.at[0])
    arrived(wsib.at[1], wrs.at[1])
    one(0, low, xall[0, 0, 0], xall[0, 0, 1], 1, wsib[0], wsib[1])
    send_products(0, low)
    arrived(xall.at[0, 1], xr.at[0, 1])
    put(xall.at[0, 1], xsib.at[0, 1], s_half, rs.at[0, 6], to_sib)
    put(xall.at[0, 1], xall.at[7, 0], s_move, xr.at[7, 0], z_up)
    put(xall.at[0, 1], xall.at[7, 1], s_move, xr.at[7, 1], z_down)
    for k, w in enumerate((wown, wsib)):
        one(0, high, xall[0, 1, 0], xall[0, 1, 1], k, w[0], w[1])
    send_products(0, high)

    def products(b):
        @pl.when(b < 5)
        def _():
            arrived(xall.at[b, 0], xr.at[b, 0])

            @pl.when(b < 4)
            def _():
                put(xall.at[b, 0], xall.at[b + 1, 0], s_move, xr.at[b + 1, 0], z_up)

            arrived(xall.at[b, 1], xr.at[b, 1])

            @pl.when(b < 3)
            def _():
                put(xall.at[b, 1], xall.at[b + 1, 1], s_move, xr.at[b + 1, 1], z_down)

        x = xall[b, :, 0].reshape(ROWS, W)
        g = xall[b, :, 1].reshape(ROWS, W)
        for k, w in enumerate((wown, wsib)):
            one(b, every, x, g, k, w[0], w[1])
        send_products(b, every)
        put(xall.at[b], xsib.at[b], s_half, rs.at[b, 6], to_sib)

    def forward(t):
        s = 8 - t
        arrived(xall.at[s, 1], xr.at[s, 1])
        put(xall.at[s, 1], xall.at[s - 1, 1], s_move, xr.at[s - 1, 1], z_down)
        arrived(xall.at[s, 0], xr.at[s, 0])

        @pl.when(t < 3)
        def _():
            put(xall.at[s, 0], xall.at[s - 1, 0], s_move, xr.at[s - 1, 0], z_up)

    def relay_sums(b):
        arrived(got.at[pl.ds(6 * b, 2)], rs.at[b, 0])
        part[b, up, 0] = (part[b, up, 0].astype(F32) + got[6 * b].astype(F32)).astype(BF16)
        put(part.at[b, up, 0], got.at[6 * b + 4], s_sum, rs.at[b, 1], to_up)
        part[b, down, 1] = (
            part[b, down, 1].astype(F32) + got[6 * b + 1].astype(F32)
        ).astype(BF16)
        put(part.at[b, down, 1], got.at[6 * b + 5], s_sum, rs.at[b, 1], to_down)

    def quarter_sums(b):
        arrived(got.at[pl.ds(6 * b + 2, 4)], rs.at[b, 1])
        part[b, yy, 0] = (
            part[b, yy, 0].astype(F32) + got[6 * b + 3].astype(F32) + got[6 * b + 4].astype(F32)
        ).astype(BF16)
        part[b, yy, 1] = (
            part[b, yy, 1].astype(F32) + got[6 * b + 2].astype(F32) + got[6 * b + 5].astype(F32)
        ).astype(BF16)
        put(part.at[b, yy], xgot.at[b], s_act, rs.at[b, 2], to_hi)

    def activate(b):
        arrived(xgot.at[b], rs.at[b, 2])
        value_out, slope = gelu_parts(part[b, yy, 0].astype(F32) + xgot[b, 0].astype(F32))
        d_pre = (part[b, yy, 1].astype(F32) + xgot[b, 1].astype(F32)) * slope
        full[b, yy, :, 0] = value_out.astype(BF16).reshape(2, HALF, Q)
        full[b, yy, :, 1] = d_pre.astype(BF16).reshape(2, HALF, Q)

        @pl.when(b < SPLIT)
        def _():
            mine = full.at[b, yy, xh]
            put(mine, mine, s_act, rs.at[b, 3], to_up)
            put(mine, mine, s_act, rs.at[b, 3], to_down)

        @pl.when(b >= SPLIT)
        def _():
            mine = full.at[b, yy]
            put(mine, mine, s_act, rs.at[b, 3], to_up)
            put(mine, mine, s_act, rs.at[b, 3], to_down)

    def relay_acts(b):
        @pl.when(b < SPLIT)
        def _():
            arrived(full.at[b, 0], rs.at[b, 3])
            low, high = full.at[b, down, xh], full.at[b, up, xh]
            put(low.at[0], low.at[0], s_pass, rs.at[b, 4], to_up)
            put(high.at[1], high.at[1], s_pass, rs.at[b, 4], to_down)
            put(low, low, s_pass, rs.at[b, 5], to_hi)
            put(high, high, s_pass, rs.at[b, 5], to_hi)

        @pl.when(b >= SPLIT)
        def _():
            arrived(full.at[b, 0:2], rs.at[b, 3])
            low, high = full.at[b, down, :, 0], full.at[b, up, :, 1]
            put(low, low, s_pass, rs.at[b, 4], to_up)
            put(high, high, s_pass, rs.at[b, 4], to_down)

    def far_acts(b):
        mine = full.at[b, far, xh]
        arrived(mine, rs.at[b, 4])
        put(mine, mine, s_pass, rs.at[b, 5], to_hi)

    def input_grad(b, ready, sem):
        arrived(ready, sem)
        put(full.at[b, 2:4], fsib.at[b], s_half, rs.at[b, 6], to_sib)
        own, sib = [
            jnp.concatenate([full[b, q, :, 1].reshape(ROWS, Q) for q in qs], axis=1)
            for qs in ((0, 1), (2, 3))
        ]
        partial = contract(own, wown[0], 1, 1) + contract(sib, wsib[0], 1, 1)

        @pl.when(b < 4)
        def _():
            dxs[b] = partial.astype(BF16)

            @pl.when(b > 0)
            def _():
                put(dxs.at[b, low], dxr.at[2 * b], s_pass, srs.at[2], {"gx": (z + 8 - b) % 8})
                put(dxs.at[b, high], dxr.at[2 * b + 1], s_pass, srs.at[2], {"gx": (z + b) % 8})

            @pl.when(b == 0)
            def _():
                put(dxs.at[0, high], dxr.at[1], s_pass, srs.at[2], to_lo)

        @pl.when(b == 4)
        def _():
            dxs[b] = partial.astype(BF16)
            put(dxs.at[4, low], dxr.at[8], s_pass, srs.at[2], {"gx": (z + 4) % 8})
            put(dxs.at[4, high], dxr.at[11], s_pass, crs.at[0, 1], z_up)

        @pl.when(b > 4)
        def _():
            arrived(dxr.at[2 * b + 1], crs.at[b - 5, 1])
            dxs[b, high] = (partial[HALF:] + dxr[2 * b + 1].astype(F32)).astype(BF16)

            @pl.when(b == 5)
            def _():
                dxs[b, low] = partial[:HALF].astype(BF16)

            @pl.when(b > 5)
            def _():
                arrived(dxr.at[2 * b], crs.at[b - 5, 0])
                dxs[b, low] = (partial[:HALF] + dxr[2 * b].astype(F32)).astype(BF16)

            @pl.when(b < NB - 1)
            def _():
                put(dxs.at[b, low], dxr.at[2 * b + 2], s_pass, crs.at[b - 4, 0], z_down)
                put(dxs.at[b, high], dxr.at[2 * b + 3], s_pass, crs.at[b - 4, 1], z_up)

            @pl.when(b == NB - 1)
            def _():
                put(
                    dxs.at[b, low], dxr.at[9], s_pass, srs.at[2],
                    {"gx": (z + 7) % 8, "gy": other_gy},
                )
                put(
                    dxs.at[b, high], dxr.at[10], s_pass, srs.at[2],
                    {"gx": (z + 1) % 8, "gy": other_gy},
                )

    def input_grad_split(b):
        input_grad(b, full.at[b, 0:3, 0], rs.at[b, 5])

    def input_grad_whole(b):
        input_grad(b, full.at[b, far], rs.at[b, 4])

    def pair(tokens, acts, first):
        x = tokens[pl.ds(first, 2), :, 0].reshape(2 * ROWS, W)
        g = tokens[pl.ds(first, 2), :, 1].reshape(2 * ROWS, W)
        act = [acts[pl.ds(first, 2), q, :, 0].reshape(2 * ROWS, Q) for q in range(2)]
        d_pre = [acts[pl.ds(first, 2), q, :, 1].reshape(2 * ROWS, Q) for q in range(2)]
        return x, g, act, d_pre

    def weight_grads(parts):
        x_t = jnp.concatenate([part[0] for part in parts], axis=0).T
        g = jnp.concatenate([part[1] for part in parts], axis=0)
        for q in range(2):
            act_t = jnp.concatenate([part[2][q] for part in parts], axis=0).T
            d_pre = jnp.concatenate([part[3][q] for part in parts], axis=0)
            acc_in[q] += contract(x_t, d_pre, 1, 0)
            acc_out[q] += contract(act_t, g, 1, 0)

    def sibling_done(b):
        arrived(got.at[0:8], rs.at[b, 6])

    stages = (
        (5, NB, 0, products), (0, NB, 1, relay_sums), (0, NB, 2, quarter_sums),
        (0, NB, 3, activate), (0, NB, 4, relay_acts), (0, SPLIT, 5, far_acts),
        (0, SPLIT, 6, input_grad_split), (SPLIT, NB, 5, input_grad_whole),
        (1, 5, 0, products),
    )

    @pl.loop(1, NB + 5)
    def _(t):
        for first, end, lag, stage in stages:
            b = t - lag

            @pl.when((b >= first) & (b < end))
            def _(stage=stage, b=b):
                stage(b)

        @pl.when(t < 4)
        def _():
            forward(t)

        last = t - 6

        @pl.when((last >= 0) & (last < NB - 1) & (last % 2 == 1))
        def _():
            sibling_done(last - 1)
            sibling_done(last)
            weight_grads([pair(xall, full, last - 1), pair(xsib, fsib, last - 1)])

    weight_grads([pair(xall, full, NB - 2)])
    sibling_done(NB - 2)
    sibling_done(NB - 1)
    weight_grads([pair(xsib, fsib, NB - 2)])

    def folded(values):
        rows = jnp.sum((values * values).reshape(-1, 8, values.shape[1]), axis=0)
        out = rows[:, 0:128]
        for i in range(1, values.shape[1] // 128):
            out += rows[:, 128 * i : 128 * (i + 1)]
        return out

    squares = jnp.zeros((8, 128), F32)
    stores = []
    for j in range(2):
        squares += folded(acc_in[j]) + folded(acc_out[j])
        stores.append(pltpu.make_async_copy(acc_in.at[j], o_gin.at[:, j * Q : (j + 1) * Q], ls.at[j]))
        stores.append(pltpu.make_async_copy(acc_out.at[j], o_gout.at[j * Q : (j + 1) * Q], ls.at[2 + j]))
    sq[0] = squares

    for slot, where in group_two:
        put(sq.at[0], sqr1.at[slot], s_one, srs.at[0], where)
    for store in stores:
        store.start()
    arrived(sqr1.at[1:16], srs.at[0])
    whole = sq[0] + jnp.sum(sqr1[1:16], axis=0)
    sq[1] = whole
    for slot, where in group_one:
        put(sq.at[1], sqr2.at[slot], s_two, srs.at[1], where)

    arrived(dxr.at[1:11], srs.at[2])
    total = dxs[0, 0:HALF].astype(F32)
    for i in range(1, 11):
        total += dxr[i].astype(F32)
    o_dx[...] = total.astype(BF16)

    arrived(sqr2.at[1:16], srs.at[1])
    o_sum[...] = whole + jnp.sum(sqr2[1:16], axis=0)

    for store in stores:
        store.wait()
    left(got.at[0:48], s_sum)
    left(got.at[0 : 16 + 2 * (16 - SPLIT)], s_act)
    left(got.at[0 : (16 - SPLIT) + 3 * SPLIT + 15], s_pass)
    left(got.at[0:30], s_move)
    left(got.at[0:24], s_core)
    left(part, s_half)
    left(sqr1.at[1:16], s_one)
    left(sqr2.at[1:16], s_two)


def scale_kernel(squares, dx, gin, gout, o_dx, o_gin, o_gout):
    total = jnp.sum(squares[...], keepdims=True)
    factor = 1.0 / jnp.sqrt(total / (2.0 * D * FW) + 1e-06)
    o_dx[...] = dx[...]
    o_gin[...] = (gin[...] * factor).astype(BF16)
    o_gout[...] = (gout[...] * factor).astype(BF16)


def scaled(squares, in_grad, grad_in, grad_out):
    steps = 4
    fixed = lambda shape: pl.BlockSpec(shape, lambda i: (0, 0))
    moving = lambda: pl.BlockSpec((W // steps, W), lambda i: (i, 0))
    return pl.pallas_call(
        scale_kernel,
        grid=(steps,),
        out_shape=(
            jax.ShapeDtypeStruct((HALF, W), BF16),
            jax.ShapeDtypeStruct((W, W), BF16),
            jax.ShapeDtypeStruct((W, W), BF16),
        ),
        in_specs=[fixed((8, 128)), fixed((HALF, W)), moving(), moving()],
        out_specs=(fixed((HALF, W)), moving(), moving()),
    )(squares, in_grad, grad_in, grad_out)


def shards(tokens, w_in, w_out, out_grad):
    vmem = pl.BlockSpec(memory_space=pltpu.VMEM)
    hbm = pl.BlockSpec(memory_space=pl.ANY)
    dma = pltpu.SemaphoreType.DMA
    in_grad, grad_in, grad_out, squares = pl.pallas_call(
        kernel,
        out_shape=(
            jax.ShapeDtypeStruct((HALF, W), BF16),
            jax.ShapeDtypeStruct((W, W), F32),
            jax.ShapeDtypeStruct((W, W), F32),
            jax.ShapeDtypeStruct((8, 128), F32),
        ),
        in_specs=[hbm] * 4,
        out_specs=(vmem, hbm, hbm, vmem),
        scratch_shapes=[
            pltpu.VMEM((NB, 2, 2, HALF, W), BF16),
            pltpu.VMEM((NB, 2, 2, HALF, W), BF16),
            pltpu.VMEM((2, W, W), BF16),
            pltpu.VMEM((2, W, W), BF16),
            pltpu.VMEM((NB, 4, 2, ROWS, Q), BF16),
            pltpu.VMEM((NB * 6, ROWS, Q), BF16),
            pltpu.VMEM((NB, 2, ROWS, Q), BF16),
            pltpu.VMEM((NB, 4, 2, 2, HALF, Q), BF16),
            pltpu.VMEM((NB, 2, 2, 2, HALF, Q), BF16),
            pltpu.VMEM((2, W, Q), F32),
            pltpu.VMEM((2, Q, W), F32),
            pltpu.VMEM((NB, ROWS, W), BF16),
            pltpu.VMEM((16, HALF, W), BF16),
            pltpu.VMEM((2, 8, 128), F32),
            pltpu.VMEM((16, 8, 128), F32),
            pltpu.VMEM((16, 8, 128), F32),
            dma((4,)),
            dma((8,)),
            dma((NB, 2)),
            dma((NB, 7)),
            dma((2,)),
            dma((3,)),
            dma((3, 2)),
        ],
        compiler_params=pltpu.CompilerParams(
            collective_id=0, has_side_effects=True, vmem_limit_bytes=60 * 2**20
        ),
        cost_estimate=pl.CostEstimate(
            flops=12_100_000_000, bytes_accessed=10_000_000, transcendentals=400_000
        ),
    )(tokens, w_in, w_out, out_grad)
    return scaled(squares, in_grad, grad_in, grad_out)


def solution(mesh):
    placed = (
        P(("gy", "gx"), "gz"),
        P("gz", ("gx", "gy")),
        P(("gx", "gy"), "gz"),
        P(("gy", "gx"), "gz"),
    )
    return jax.shard_map(
        shards,
        mesh=mesh,
        in_specs=placed,
        out_specs=(P(("gy", "gx"), "gz"), P("gz", ("gx", "gy")), P(("gx", "gy"), "gz")),
        check_vma=False,
    )
```

```python
import jax
import jax.numpy as jnp
from jax import lax
from jax.experimental import pallas as pl
from jax.experimental.pallas import tpu as pltpu
from jax.sharding import PartitionSpec as P

D = 6144
FW = 24576
GELU_C = 0.7978845608
MESH = pl.DeviceIdType.MESH

NB = 16
ROWS = 64
HALF = 32
W = 768
SPLIT, EVERY, OF = 14, 2, 1
Q = 384
F32 = jnp.float32
BF16 = jnp.bfloat16


def gelu_parts(values):
    square = values * values
    inner_arg = GELU_C * (values + 0.044715 * square * values)
    tanh_val = jnp.tanh(inner_arg)
    value_out = 0.5 * values * (1.0 + tanh_val)
    slope = 0.5 * (1.0 + tanh_val) + 0.5 * values * (1.0 - tanh_val * tanh_val) * GELU_C * (
        1.0 + 3.0 * 0.044715 * square
    )
    return (value_out, slope)


def contract(left, right, left_dim, right_dim):
    return lax.dot_general(
        left, right, (((left_dim,), (right_dim,)), ((), ())), preferred_element_type=F32
    )


def kernel(
    tok, win, wout, dy, o_dx, o_gin, o_gout, o_sum,
    xall, xsib, wown, wsib, part, got, xgot, full, fsib, acc_in, acc_out, out_in, out_out, dxs, dxr,
    sq, sqr1, sqr2,
    ls, ss, xr, rs, wrs, srs, crs,
):
    z, gy, gz = lax.axis_index("gx"), lax.axis_index("gy"), lax.axis_index("gz")
    yy, xh = gz // 2, gz % 2
    xl, core = gy // 2, gy % 2
    up, down, far = (yy + 1) % 4, (yy + 3) % 4, (yy + 2) % 4
    to_up, to_down = {"gz": up * 2 + xh}, {"gz": down * 2 + xh}
    hi_gz = yy * 2 + 1 - xh
    other_gy = (1 - xl) * 2 + core
    sib_gy = xl * 2 + 1 - core
    to_hi, to_lo, to_sib = {"gz": hi_gz}, {"gy": other_gy}, {"gy": sib_gy}
    z_up, z_down = {"gx": (z + 1) % 8}, {"gx": (z + 7) % 8}

    group_one = [
        (dz * 2 + k, {"gx": (z + dz) % 8, "gy": other_gy if k else gy})
        for dz in range(8) for k in range(2) if dz + k
    ]
    group_two = [
        (d * 4 + kx * 2 + kc, {
            "gz": ((yy + d) % 4) * 2 + (1 - xh if kx else xh),
            "gy": sib_gy if kc else gy,
        })
        for d in range(4) for kx in range(2) for kc in range(2) if d + kx + kc
    ]
    s_sum, s_act, s_pass, s_move, s_core, s_one, s_two, s_half = [ss.at[i] for i in range(8)]

    def put(src, dst, send, recv, where):
        pltpu.make_async_remote_copy(
            src_ref=src, dst_ref=dst, send_sem=send, recv_sem=recv,
            device_id=where, device_id_type=MESH,
        ).start()

    def arrived(ref, sem):
        pltpu.make_async_remote_copy(
            src_ref=ref, dst_ref=ref, send_sem=sem, recv_sem=sem,
            device_id=to_up, device_id_type=MESH,
        ).wait_recv()

    def left(ref, sem):
        pltpu.make_async_remote_copy(
            src_ref=ref, dst_ref=ref, send_sem=sem, recv_sem=sem,
            device_id=to_up, device_id_type=MESH,
        ).wait_send()

    loads = [
        pltpu.make_async_copy(tok, xall.at[0, 0, 0], ls.at[0]),
        pltpu.make_async_copy(dy, xall.at[0, 0, 1], ls.at[1]),
        pltpu.make_async_copy(win, wown.at[0], ls.at[2]),
        pltpu.make_async_copy(wout, wown.at[1], ls.at[3]),
    ]
    for load in loads:
        load.start()
    barrier = pltpu.get_barrier_semaphore()
    for _, where in group_one + group_two:
        pl.semaphore_signal(barrier, inc=1, device_id=where, device_id_type=MESH)
    acc_in[...] = jnp.zeros_like(acc_in)
    acc_out[...] = jnp.zeros_like(acc_out)
    loads[0].wait()
    loads[1].wait()
    pl.semaphore_wait(barrier, 30)

    put(xall.at[0, 0], xall.at[0, 1], s_move, xr.at[0, 1], to_lo)
    put(xall.at[0, 0], xall.at[1, 0], s_move, xr.at[1, 0], z_up)
    put(xall.at[0, 0], xall.at[1, 1], s_move, xr.at[1, 1], z_down)
    loads[2].wait()
    loads[3].wait()
    put(wown.at[0], wsib.at[0], s_core, wrs.at[0], to_sib)
    put(wown.at[1], wsib.at[1], s_core, wrs.at[1], to_sib)

    def one(b, x, g, which, w_in, w_out):
        h = contract(x, w_in, 1, 0).astype(BF16)
        part[b, 2 * which, 0] = h[:, :Q]
        part[b, 2 * which + 1, 0] = h[:, Q:]
        d = contract(g, w_out, 1, 1).astype(BF16)
        part[b, 2 * which, 1] = d[:, :Q]
        part[b, 2 * which + 1, 1] = d[:, Q:]

    def send_products(b):
        put(part.at[b, far, 0], got.at[6 * b], s_sum, rs.at[b, 0], to_up)
        put(part.at[b, far, 1], got.at[6 * b + 1], s_sum, rs.at[b, 0], to_down)
        put(part.at[b, up, 1], got.at[6 * b + 2], s_sum, rs.at[b, 1], to_up)
        put(part.at[b, down, 0], got.at[6 * b + 3], s_sum, rs.at[b, 1], to_down)

    put(xall.at[0, 0], xsib.at[0, 0], s_half, rs.at[0, 6], to_sib)
    one(0, xall[0, 0, 0], xall[0, 0, 1], 0, wown[0], wown[1])
    arrived(wsib.at[0], wrs.at[0])
    arrived(wsib.at[1], wrs.at[1])
    one(0, xall[0, 0, 0], xall[0, 0, 1], 1, wsib[0], wsib[1])
    send_products(0)

    def products(b):
        slot, side = b // 2, b % 2

        @pl.when(b < 10)
        def _():
            arrived(xall.at[slot, side], xr.at[slot, side])

        @pl.when((b > 1) & (b < 8) & (side == 0))
        def _():
            put(xall.at[slot, 0], xall.at[slot + 1, 0], s_move, xr.at[slot + 1, 0], z_up)

        @pl.when((b > 1) & (b < 6) & (side == 1))
        def _():
            put(xall.at[slot, 1], xall.at[slot + 1, 1], s_move, xr.at[slot + 1, 1], z_down)

        @pl.when(b == 8)
        def _():
            put(xall.at[4, 0], xall.at[4, 1], s_move, xr.at[4, 1], to_lo)

        for k, w in enumerate((wown, wsib)):
            one(b, xall[slot, side, 0], xall[slot, side, 1], k, w[0], w[1])
        send_products(b)
        put(xall.at[slot, side], xsib.at[slot, side], s_half, rs.at[b, 6], to_sib)

    def forward(s):
        arrived(xall.at[s, 0], xr.at[s, 0])
        put(xall.at[s, 0], xall.at[s - 1, 0], s_move, xr.at[s - 1, 0], z_up)
        arrived(xall.at[s, 1], xr.at[s, 1])
        put(xall.at[s, 1], xall.at[s - 1, 1], s_move, xr.at[s - 1, 1], z_down)

    def relay_sums(b):
        arrived(got.at[pl.ds(6 * b, 2)], rs.at[b, 0])
        part[b, up, 0] = (part[b, up, 0].astype(F32) + got[6 * b].astype(F32)).astype(BF16)
        put(part.at[b, up, 0], got.at[6 * b + 4], s_sum, rs.at[b, 1], to_up)
        part[b, down, 1] = (
            part[b, down, 1].astype(F32) + got[6 * b + 1].astype(F32)
        ).astype(BF16)
        put(part.at[b, down, 1], got.at[6 * b + 5], s_sum, rs.at[b, 1], to_down)

    def quarter_sums(b):
        arrived(got.at[pl.ds(6 * b + 2, 4)], rs.at[b, 1])
        part[b, yy, 0] = (
            part[b, yy, 0].astype(F32) + got[6 * b + 3].astype(F32) + got[6 * b + 4].astype(F32)
        ).astype(BF16)
        part[b, yy, 1] = (
            part[b, yy, 1].astype(F32) + got[6 * b + 2].astype(F32) + got[6 * b + 5].astype(F32)
        ).astype(BF16)
        put(part.at[b, yy], xgot.at[b], s_act, rs.at[b, 2], to_hi)

    def in_split(b):
        return (b < SPLIT) & (b % EVERY < OF)

    def activate(b):
        arrived(xgot.at[b], rs.at[b, 2])
        value_out, slope = gelu_parts(part[b, yy, 0].astype(F32) + xgot[b, 0].astype(F32))
        d_pre = (part[b, yy, 1].astype(F32) + xgot[b, 1].astype(F32)) * slope
        full[b, yy, :, 0] = value_out.astype(BF16).reshape(2, HALF, Q)
        full[b, yy, :, 1] = d_pre.astype(BF16).reshape(2, HALF, Q)

        @pl.when(in_split(b))
        def _():
            mine = full.at[b, yy, xh]
            put(mine, mine, s_act, rs.at[b, 3], to_up)
            put(mine, mine, s_act, rs.at[b, 3], to_down)

        @pl.when(jnp.logical_not(in_split(b)))
        def _():
            mine = full.at[b, yy]
            put(mine, mine, s_act, rs.at[b, 3], to_up)
            put(mine, mine, s_act, rs.at[b, 3], to_down)

    def relay_acts(b):
        @pl.when(in_split(b))
        def _():
            arrived(full.at[b, 0], rs.at[b, 3])
            low, high = full.at[b, down, xh], full.at[b, up, xh]
            put(low.at[0], low.at[0], s_pass, rs.at[b, 4], to_up)
            put(high.at[1], high.at[1], s_pass, rs.at[b, 4], to_down)
            put(low, low, s_pass, rs.at[b, 5], to_hi)
            put(high, high, s_pass, rs.at[b, 5], to_hi)

        @pl.when(jnp.logical_not(in_split(b)))
        def _():
            arrived(full.at[b, 0:2], rs.at[b, 3])
            low, high = full.at[b, down, :, 0], full.at[b, up, :, 1]
            put(low, low, s_pass, rs.at[b, 4], to_up)
            put(high, high, s_pass, rs.at[b, 4], to_down)

    def far_acts(b):
        mine = full.at[b, far, xh]
        arrived(mine, rs.at[b, 4])
        put(mine, mine, s_pass, rs.at[b, 5], to_hi)

    def acts_ready(b, ready, sem):
        arrived(ready, sem)
        put(full.at[b, 2:4], fsib.at[b], s_half, rs.at[b, 6], to_sib)

    def input_grad(b):
        own, sib = [
            jnp.concatenate([full[b, q, :, 1].reshape(ROWS, Q) for q in qs], axis=1)
            for qs in ((0, 1), (2, 3))
        ]
        partial = contract(own, wown[0], 1, 1) + contract(sib, wsib[0], 1, 1)

        slot, side = b // 2, b % 2

        @pl.when(b < 8)
        def _():
            dxs[b] = partial.astype(BF16)

            @pl.when((b > 1) & (side == 0))
            def _():
                put(dxs.at[b], dxr.at[b], s_pass, srs.at[2], {"gx": (z + 8 - slot) % 8})

            @pl.when((b > 1) & (side == 1))
            def _():
                put(dxs.at[b], dxr.at[b], s_pass, srs.at[2], {"gx": (z + slot) % 8})

            @pl.when(b == 1)
            def _():
                put(dxs.at[1], dxr.at[1], s_pass, srs.at[2], to_lo)

        @pl.when(b == 8)
        def _():
            dxs[b] = partial.astype(BF16)
            put(dxs.at[8], dxr.at[8], s_pass, srs.at[2], {"gx": (z + 4) % 8})

        @pl.when((b == 9) | (b == 10))
        def _():
            dxs[b] = partial.astype(BF16)

        @pl.when(b > 10)
        def _():
            arrived(dxr.at[b], crs.at[b - 11])
            dxs[b] = (partial + dxr[b].astype(F32)).astype(BF16)

        @pl.when((b > 8) & (b < NB - 2) & (side == 0))
        def _():
            put(dxs.at[b], dxr.at[b + 2], s_pass, crs.at[b - 9], z_down)

        @pl.when((b > 8) & (b < NB - 2) & (side == 1))
        def _():
            put(dxs.at[b], dxr.at[b + 2], s_pass, crs.at[b - 9], z_up)

        @pl.when(b == NB - 2)
        def _():
            put(dxs.at[b], dxr.at[9], s_pass, srs.at[2], {"gx": (z + 7) % 8, "gy": other_gy})

        @pl.when(b == NB - 1)
        def _():
            put(dxs.at[b], dxr.at[10], s_pass, srs.at[2], {"gx": (z + 1) % 8, "gy": other_gy})

    def input_grad_split(b):
        acts_ready(b, full.at[b, 0:3, 0], rs.at[b, 5])
        input_grad(b)

    def input_grad_whole(b):
        acts_ready(b, full.at[b, far], rs.at[b, 4])
        input_grad(b)

    def blocks(tokens, acts, first, count):
        if count > 1:
            slots = pl.ds(first // 2, count // 2)
            x = tokens[slots, :, 0].reshape(count * ROWS, W)
            g = tokens[slots, :, 1].reshape(count * ROWS, W)
        else:
            x, g = tokens[first // 2, first % 2, 0], tokens[first // 2, first % 2, 1]
        act = [acts[pl.ds(first, count), q, :, 0].reshape(count * ROWS, Q) for q in range(2)]
        d_pre = [acts[pl.ds(first, count), q, :, 1].reshape(count * ROWS, Q) for q in range(2)]
        return x, g, act, d_pre

    def weight_grads(parts):
        x_t = jnp.concatenate([part[0] for part in parts], axis=0).T
        g = jnp.concatenate([part[1] for part in parts], axis=0)
        for q in range(2):
            act_t = jnp.concatenate([part[2][q] for part in parts], axis=0).T
            d_pre = jnp.concatenate([part[3][q] for part in parts], axis=0)
            acc_in[q] += contract(x_t, d_pre, 1, 0)
            acc_out[q] += contract(act_t, g, 1, 0)

    def sibling_done(b):
        arrived(got.at[0:8], rs.at[b, 6])

    stages = (
        (1, NB, None, 0, products), (0, NB, None, 1, relay_sums), (0, NB, None, 2, quarter_sums),
        (0, NB, None, 3, activate), (0, NB, None, 4, relay_acts), (0, NB, True, 5, far_acts),
        (0, NB, True, 6, input_grad_split), (0, NB - 1, False, 5, input_grad_whole),
    )

    @pl.loop(1, NB + 4)
    def _(t):
        for first, end, split, lag, stage in stages:
            b = t - lag
            runs = (b >= first) & (b < end)
            if split is not None:
                runs = runs & (in_split(b) if split else jnp.logical_not(in_split(b)))

            @pl.when(runs)
            def _(stage=stage, b=b):
                stage(b)

        @pl.when(t == 3)
        def _():
            put(xall.at[0, 1], xall.at[7, 0], s_move, xr.at[7, 0], z_up)
            put(xall.at[0, 1], xall.at[7, 1], s_move, xr.at[7, 1], z_down)

        @pl.when((t == 5) | (t == 7))
        def _():
            forward(7 - (t - 5) // 2)

        @pl.when(t == 9)
        def _():
            arrived(xall.at[5, 0], xr.at[5, 0])
            arrived(xall.at[5, 1], xr.at[5, 1])

        last = t - 6

        @pl.when((last >= 0) & (last < NB - 4) & (last % 4 == 3))
        def _():
            for i in range(4):
                sibling_done(last - i)
            weight_grads([blocks(xall, full, last - 3, 4), blocks(xsib, fsib, last - 3, 4)])

    sibling_done(NB - 4)
    sibling_done(NB - 3)
    weight_grads([blocks(xall, full, NB - 4, 2), blocks(xsib, fsib, NB - 4, 2)])
    sibling_done(NB - 2)
    weight_grads([blocks(xall, full, NB - 2, 1), blocks(xsib, fsib, NB - 2, 1)])
    acts_ready(NB - 1, full.at[NB - 1, far], rs.at[NB - 1, 4])
    sibling_done(NB - 1)
    weight_grads([blocks(xall, full, NB - 1, 1), blocks(xsib, fsib, NB - 1, 1)])

    def folded(values):
        rows = jnp.sum((values * values).reshape(-1, 8, values.shape[1]), axis=0)
        out = rows[:, 0:128]
        for i in range(1, values.shape[1] // 128):
            out += rows[:, 128 * i : 128 * (i + 1)]
        return out

    squares = jnp.zeros((8, 128), F32)
    stores = []
    for j in range(2):
        squares += folded(acc_in[j]) + folded(acc_out[j])
    sq[0] = squares

    for slot, where in group_two:
        put(sq.at[0], sqr1.at[slot], s_one, srs.at[0], where)
    for j in range(2):
        out_in[j] = acc_in[j].astype(BF16)
        out_out[j] = acc_out[j].astype(BF16)
        stores.append(pltpu.make_async_copy(out_in.at[j], o_gin.at[:, j * Q : (j + 1) * Q], ls.at[j]))
        stores.append(pltpu.make_async_copy(out_out.at[j], o_gout.at[j * Q : (j + 1) * Q], ls.at[2 + j]))
    for store in stores:
        store.start()
    input_grad(jnp.int32(NB - 1))
    arrived(sqr1.at[1:16], srs.at[0])
    whole = sq[0] + jnp.sum(sqr1[1:16], axis=0)
    sq[1] = whole
    for slot, where in group_one:
        put(sq.at[1], sqr2.at[slot], s_two, srs.at[1], where)

    arrived(dxr.at[1:11], srs.at[2])
    total = dxs[0].astype(F32)
    for i in range(1, 11):
        total += dxr[i].astype(F32)
    o_dx[...] = total.astype(BF16)

    arrived(sqr2.at[1:16], srs.at[1])
    o_sum[...] = whole + jnp.sum(sqr2[1:16], axis=0)

    for store in stores:
        store.wait()
    split = sum(1 for b in range(SPLIT) if b % EVERY < OF)
    left(got, s_sum)
    left(got.at[0 : 96 - 2 * split], s_act)
    left(got.at[0 : 62 + 2 * split], s_pass)
    left(got.at[0:60], s_move)
    left(got.at[0:48], s_core)
    left(part, s_half)
    left(sqr1.at[1:16], s_one)
    left(sqr2.at[1:16], s_two)


def scale_kernel(squares, dx, gin, gout, o_dx, o_gin, o_gout):
    total = jnp.sum(squares[...], keepdims=True)
    factor = 1.0 / jnp.sqrt(total / (2.0 * D * FW) + 1e-06)
    o_dx[...] = dx[...]
    o_gin[...] = (gin[...].astype(F32) * factor).astype(BF16)
    o_gout[...] = (gout[...].astype(F32) * factor).astype(BF16)


def scaled(squares, in_grad, grad_in, grad_out):
    steps = 4
    fixed = lambda shape: pl.BlockSpec(shape, lambda i: (0, 0))
    moving = lambda: pl.BlockSpec((W // steps, W), lambda i: (i, 0))
    return pl.pallas_call(
        scale_kernel,
        grid=(steps,),
        out_shape=(
            jax.ShapeDtypeStruct((ROWS, W), BF16),
            jax.ShapeDtypeStruct((W, W), BF16),
            jax.ShapeDtypeStruct((W, W), BF16),
        ),
        in_specs=[fixed((8, 128)), fixed((ROWS, W)), moving(), moving()],
        out_specs=(fixed((ROWS, W)), moving(), moving()),
    )(squares, in_grad, grad_in, grad_out)


def shards(tokens, w_in, w_out, out_grad):
    vmem = pl.BlockSpec(memory_space=pltpu.VMEM)
    hbm = pl.BlockSpec(memory_space=pl.ANY)
    dma = pltpu.SemaphoreType.DMA
    in_grad, grad_in, grad_out, squares = pl.pallas_call(
        kernel,
        out_shape=(
            jax.ShapeDtypeStruct((ROWS, W), BF16),
            jax.ShapeDtypeStruct((W, W), BF16),
            jax.ShapeDtypeStruct((W, W), BF16),
            jax.ShapeDtypeStruct((8, 128), F32),
        ),
        in_specs=[hbm] * 4,
        out_specs=(vmem, hbm, hbm, vmem),
        scratch_shapes=[
            pltpu.VMEM((NB // 2, 2, 2, ROWS, W), BF16),
            pltpu.VMEM((NB // 2, 2, 2, ROWS, W), BF16),
            pltpu.VMEM((2, W, W), BF16),
            pltpu.VMEM((2, W, W), BF16),
            pltpu.VMEM((NB, 4, 2, ROWS, Q), BF16),
            pltpu.VMEM((NB * 6, ROWS, Q), BF16),
            pltpu.VMEM((NB, 2, ROWS, Q), BF16),
            pltpu.VMEM((NB, 4, 2, 2, HALF, Q), BF16),
            pltpu.VMEM((NB, 2, 2, 2, HALF, Q), BF16),
            pltpu.VMEM((2, W, Q), F32),
            pltpu.VMEM((2, Q, W), F32),
            pltpu.VMEM((2, W, Q), BF16),
            pltpu.VMEM((2, Q, W), BF16),
            pltpu.VMEM((NB, ROWS, W), BF16),
            pltpu.VMEM((16, ROWS, W), BF16),
            pltpu.VMEM((2, 8, 128), F32),
            pltpu.VMEM((16, 8, 128), F32),
            pltpu.VMEM((16, 8, 128), F32),
            dma((4,)),
            dma((8,)),
            dma((NB // 2, 2)),
            dma((NB, 7)),
            dma((2,)),
            dma((3,)),
            dma((5,)),
        ],
        compiler_params=pltpu.CompilerParams(
            collective_id=0, has_side_effects=True, vmem_limit_bytes=60 * 2**20
        ),
        cost_estimate=pl.CostEstimate(
            flops=12_100_000_000, bytes_accessed=10_000_000, transcendentals=400_000
        ),
    )(tokens, w_in, w_out, out_grad)
    return scaled(squares, in_grad, grad_in, grad_out)


def solution(mesh):
    placed = (
        P(("gy", "gx"), "gz"),
        P("gz", ("gx", "gy")),
        P(("gx", "gy"), "gz"),
        P(("gy", "gx"), "gz"),
    )
    return jax.shard_map(
        shards,
        mesh=mesh,
        in_specs=placed,
        out_specs=(P(("gy", "gx"), "gz"), P("gz", ("gx", "gy")), P(("gx", "gy"), "gz")),
        check_vma=False,
    )
```

```python
import jax
import jax.numpy as jnp
from jax import lax
from jax.experimental import pallas as pl
from jax.experimental.pallas import tpu as pltpu
from jax.sharding import PartitionSpec as P

D = 6144
FW = 24576
GELU_C = 0.7978845608
MESH = pl.DeviceIdType.MESH

NB = 16
ROWS = 64
HALF = 32
W = 768
SPLIT, EVERY, OF = 14, 2, 1
Q = 384
F32 = jnp.float32
BF16 = jnp.bfloat16


def gelu_parts(values):
    square = values * values
    inner_arg = GELU_C * (values + 0.044715 * square * values)
    tanh_val = jnp.tanh(inner_arg)
    value_out = 0.5 * values * (1.0 + tanh_val)
    slope = 0.5 * (1.0 + tanh_val) + 0.5 * values * (1.0 - tanh_val * tanh_val) * GELU_C * (
        1.0 + 3.0 * 0.044715 * square
    )
    return (value_out, slope)


def contract(left, right, left_dim, right_dim):
    return lax.dot_general(
        left, right, (((left_dim,), (right_dim,)), ((), ())), preferred_element_type=F32
    )


def kernel(
    tok, win, wout, dy, o_dx, o_gin, o_gout, o_sum,
    xall, xsib, wown, wsib, part, got, xgot, full, fsib, acc_in, acc_out, out_in, out_out, dxs, dxr,
    sq, sqr1, sqr2,
    ls, ss, xr, rs, wrs, srs, crs,
):
    z, gy, gz = lax.axis_index("gx"), lax.axis_index("gy"), lax.axis_index("gz")
    yy, xh = gz // 2, gz % 2
    xl, core = gy // 2, gy % 2
    up, down, far = (yy + 1) % 4, (yy + 3) % 4, (yy + 2) % 4
    to_up, to_down = {"gz": up * 2 + xh}, {"gz": down * 2 + xh}
    hi_gz = yy * 2 + 1 - xh
    other_gy = (1 - xl) * 2 + core
    sib_gy = xl * 2 + 1 - core
    to_hi, to_lo, to_sib = {"gz": hi_gz}, {"gy": other_gy}, {"gy": sib_gy}
    z_up, z_down = {"gx": (z + 1) % 8}, {"gx": (z + 7) % 8}

    group_one = [
        (dz * 2 + k, {"gx": (z + dz) % 8, "gy": other_gy if k else gy})
        for dz in range(8) for k in range(2) if dz + k
    ]
    group_two = [
        (d * 4 + kx * 2 + kc, {
            "gz": ((yy + d) % 4) * 2 + (1 - xh if kx else xh),
            "gy": sib_gy if kc else gy,
        })
        for d in range(4) for kx in range(2) for kc in range(2) if d + kx + kc
    ]
    s_sum, s_act, s_pass, s_move, s_core, s_one, s_two, s_half = [ss.at[i] for i in range(8)]

    def put(src, dst, send, recv, where):
        pltpu.make_async_remote_copy(
            src_ref=src, dst_ref=dst, send_sem=send, recv_sem=recv,
            device_id=where, device_id_type=MESH,
        ).start()

    def arrived(ref, sem):
        pltpu.make_async_remote_copy(
            src_ref=ref, dst_ref=ref, send_sem=sem, recv_sem=sem,
            device_id=to_up, device_id_type=MESH,
        ).wait_recv()

    def left(ref, sem):
        pltpu.make_async_remote_copy(
            src_ref=ref, dst_ref=ref, send_sem=sem, recv_sem=sem,
            device_id=to_up, device_id_type=MESH,
        ).wait_send()

    loads = [
        pltpu.make_async_copy(tok, xall.at[0, 0, 0], ls.at[0]),
        pltpu.make_async_copy(dy, xall.at[0, 0, 1], ls.at[1]),
        pltpu.make_async_copy(win, wown.at[0], ls.at[2]),
        pltpu.make_async_copy(wout, wown.at[1], ls.at[3]),
    ]
    for load in loads:
        load.start()
    barrier = pltpu.get_barrier_semaphore()
    for _, where in group_one + group_two:
        pl.semaphore_signal(barrier, inc=1, device_id=where, device_id_type=MESH)
    acc_in[...] = jnp.zeros_like(acc_in)
    acc_out[...] = jnp.zeros_like(acc_out)
    loads[0].wait()
    loads[1].wait()
    pl.semaphore_wait(barrier, 30)

    put(xall.at[0, 0], xall.at[0, 1], s_move, xr.at[0, 1], to_lo)
    put(xall.at[0, 0], xall.at[1, 0], s_move, xr.at[1, 0], z_up)
    put(xall.at[0, 0], xall.at[1, 1], s_move, xr.at[1, 1], z_down)
    loads[2].wait()
    loads[3].wait()
    put(wown.at[0], wsib.at[0], s_core, wrs.at[0], to_sib)
    put(wown.at[1], wsib.at[1], s_core, wrs.at[1], to_sib)

    def one(b, x, g, which, w_in, w_out):
        h = contract(x, w_in, 1, 0).astype(BF16)
        part[b, 2 * which, 0] = h[:, :Q]
        part[b, 2 * which + 1, 0] = h[:, Q:]
        d = contract(g, w_out, 1, 1).astype(BF16)
        part[b, 2 * which, 1] = d[:, :Q]
        part[b, 2 * which + 1, 1] = d[:, Q:]

    def send_products(b):
        put(part.at[b, far, 0], got.at[6 * b], s_sum, rs.at[b, 0], to_up)
        put(part.at[b, far, 1], got.at[6 * b + 1], s_sum, rs.at[b, 0], to_down)
        put(part.at[b, up, 1], got.at[6 * b + 2], s_sum, rs.at[b, 1], to_up)
        put(part.at[b, down, 0], got.at[6 * b + 3], s_sum, rs.at[b, 1], to_down)

    put(xall.at[0, 0], xsib.at[0, 0], s_half, rs.at[0, 6], to_sib)
    one(0, xall[0, 0, 0], xall[0, 0, 1], 0, wown[0], wown[1])
    arrived(wsib.at[0], wrs.at[0])
    arrived(wsib.at[1], wrs.at[1])
    one(0, xall[0, 0, 0], xall[0, 0, 1], 1, wsib[0], wsib[1])
    send_products(0)

    def products(b):
        slot, side = b // 2, b % 2

        @pl.when(b < 10)
        def _():
            arrived(xall.at[slot, side], xr.at[slot, side])

        @pl.when((b > 1) & (b < 8) & (side == 0))
        def _():
            put(xall.at[slot, 0], xall.at[slot + 1, 0], s_move, xr.at[slot + 1, 0], z_up)

        @pl.when((b > 1) & (b < 6) & (side == 1))
        def _():
            put(xall.at[slot, 1], xall.at[slot + 1, 1], s_move, xr.at[slot + 1, 1], z_down)

        @pl.when(b == 8)
        def _():
            put(xall.at[4, 0], xall.at[4, 1], s_move, xr.at[4, 1], to_lo)

        for k, w in enumerate((wown, wsib)):
            one(b, xall[slot, side, 0], xall[slot, side, 1], k, w[0], w[1])
        send_products(b)
        put(xall.at[slot, side], xsib.at[slot, side], s_half, rs.at[b, 6], to_sib)

    def forward(s):
        arrived(xall.at[s, 0], xr.at[s, 0])
        put(xall.at[s, 0], xall.at[s - 1, 0], s_move, xr.at[s - 1, 0], z_up)
        arrived(xall.at[s, 1], xr.at[s, 1])
        put(xall.at[s, 1], xall.at[s - 1, 1], s_move, xr.at[s - 1, 1], z_down)

    def relay_sums(b):
        arrived(got.at[pl.ds(6 * b, 2)], rs.at[b, 0])
        part[b, up, 0] = (part[b, up, 0].astype(F32) + got[6 * b].astype(F32)).astype(BF16)
        put(part.at[b, up, 0], got.at[6 * b + 4], s_sum, rs.at[b, 1], to_up)
        part[b, down, 1] = (
            part[b, down, 1].astype(F32) + got[6 * b + 1].astype(F32)
        ).astype(BF16)
        put(part.at[b, down, 1], got.at[6 * b + 5], s_sum, rs.at[b, 1], to_down)

    def quarter_sums(b):
        arrived(got.at[pl.ds(6 * b + 2, 4)], rs.at[b, 1])
        part[b, yy, 0] = (
            part[b, yy, 0].astype(F32) + got[6 * b + 3].astype(F32) + got[6 * b + 4].astype(F32)
        ).astype(BF16)
        part[b, yy, 1] = (
            part[b, yy, 1].astype(F32) + got[6 * b + 2].astype(F32) + got[6 * b + 5].astype(F32)
        ).astype(BF16)
        put(part.at[b, yy], xgot.at[b], s_act, rs.at[b, 2], to_hi)

    def in_split(b):
        return (b < SPLIT) & (b % EVERY < OF)

    def activate(b):
        arrived(xgot.at[b], rs.at[b, 2])
        value_out, slope = gelu_parts(part[b, yy, 0].astype(F32) + xgot[b, 0].astype(F32))
        d_pre = (part[b, yy, 1].astype(F32) + xgot[b, 1].astype(F32)) * slope
        full[b, yy, :, 0] = value_out.astype(BF16).reshape(2, HALF, Q)
        full[b, yy, :, 1] = d_pre.astype(BF16).reshape(2, HALF, Q)

        @pl.when(in_split(b))
        def _():
            mine = full.at[b, yy, xh]
            put(mine, mine, s_act, rs.at[b, 3], to_up)
            put(mine, mine, s_act, rs.at[b, 3], to_down)

        @pl.when(jnp.logical_not(in_split(b)))
        def _():
            mine = full.at[b, yy]
            put(mine, mine, s_act, rs.at[b, 3], to_up)
            put(mine, mine, s_act, rs.at[b, 3], to_down)

    def relay_acts(b):
        @pl.when(in_split(b))
        def _():
            arrived(full.at[b, 0], rs.at[b, 3])
            low, high = full.at[b, down, xh], full.at[b, up, xh]
            put(low.at[0], low.at[0], s_pass, rs.at[b, 4], to_up)
            put(high.at[1], high.at[1], s_pass, rs.at[b, 4], to_down)
            put(low, low, s_pass, rs.at[b, 5], to_hi)
            put(high, high, s_pass, rs.at[b, 5], to_hi)

        @pl.when(jnp.logical_not(in_split(b)))
        def _():
            arrived(full.at[b, 0:2], rs.at[b, 3])
            low, high = full.at[b, down, :, 0], full.at[b, up, :, 1]
            put(low, low, s_pass, rs.at[b, 4], to_up)
            put(high, high, s_pass, rs.at[b, 4], to_down)

    def far_acts(b):
        mine = full.at[b, far, xh]
        arrived(mine, rs.at[b, 4])
        put(mine, mine, s_pass, rs.at[b, 5], to_hi)

    def acts_ready(b, ready, sem):
        arrived(ready, sem)
        put(full.at[b, 2:4], fsib.at[b], s_half, rs.at[b, 6], to_sib)

    def input_grad(b):
        own, sib = [
            jnp.concatenate([full[b, q, :, 1].reshape(ROWS, Q) for q in qs], axis=1)
            for qs in ((0, 1), (2, 3))
        ]
        partial = contract(own, wown[0], 1, 1) + contract(sib, wsib[0], 1, 1)

        slot, side = b // 2, b % 2

        @pl.when(b < 8)
        def _():
            dxs[b] = partial.astype(BF16)

            @pl.when((b > 1) & (side == 0))
            def _():
                put(dxs.at[b], dxr.at[b], s_pass, srs.at[2], {"gx": (z + 8 - slot) % 8})

            @pl.when((b > 1) & (side == 1))
            def _():
                put(dxs.at[b], dxr.at[b], s_pass, srs.at[2], {"gx": (z + slot) % 8})

            @pl.when(b == 1)
            def _():
                put(dxs.at[1], dxr.at[1], s_pass, srs.at[2], to_lo)

        @pl.when(b == 8)
        def _():
            dxs[b] = partial.astype(BF16)
            put(dxs.at[8], dxr.at[8], s_pass, srs.at[2], {"gx": (z + 4) % 8})

        @pl.when((b == 9) | (b == 10))
        def _():
            dxs[b] = partial.astype(BF16)

        @pl.when(b > 10)
        def _():
            arrived(dxr.at[b], crs.at[b - 11])
            dxs[b] = (partial + dxr[b].astype(F32)).astype(BF16)

        @pl.when((b > 8) & (b < NB - 2) & (side == 0))
        def _():
            put(dxs.at[b], dxr.at[b + 2], s_pass, crs.at[b - 9], z_down)

        @pl.when((b > 8) & (b < NB - 2) & (side == 1))
        def _():
            put(dxs.at[b], dxr.at[b + 2], s_pass, crs.at[b - 9], z_up)

        @pl.when(b == NB - 2)
        def _():
            put(dxs.at[b], dxr.at[9], s_pass, srs.at[2], {"gx": (z + 7) % 8, "gy": other_gy})

        @pl.when(b == NB - 1)
        def _():
            put(dxs.at[b], dxr.at[10], s_pass, srs.at[2], {"gx": (z + 1) % 8, "gy": other_gy})

    def input_grad_split(b):
        acts_ready(b, full.at[b, 0:3, 0], rs.at[b, 5])
        input_grad(b)

    def input_grad_whole(b):
        acts_ready(b, full.at[b, far], rs.at[b, 4])
        input_grad(b)

    def blocks(tokens, acts, first, count):
        if count > 1:
            slots = pl.ds(first // 2, count // 2)
            x = tokens[slots, :, 0].reshape(count * ROWS, W)
            g = tokens[slots, :, 1].reshape(count * ROWS, W)
        else:
            x, g = tokens[first // 2, first % 2, 0], tokens[first // 2, first % 2, 1]
        act = [acts[pl.ds(first, count), q, :, 0].reshape(count * ROWS, Q) for q in range(2)]
        d_pre = [acts[pl.ds(first, count), q, :, 1].reshape(count * ROWS, Q) for q in range(2)]
        return x, g, act, d_pre

    def weight_grads(parts):
        x_t = jnp.concatenate([part[0] for part in parts], axis=0).T
        g = jnp.concatenate([part[1] for part in parts], axis=0)
        for q in range(2):
            act_t = jnp.concatenate([part[2][q] for part in parts], axis=0).T
            d_pre = jnp.concatenate([part[3][q] for part in parts], axis=0)
            acc_in[q] += contract(x_t, d_pre, 1, 0)
            acc_out[q] += contract(act_t, g, 1, 0)

    def sibling_done(b):
        arrived(got.at[0:8], rs.at[b, 6])

    stages = (
        (1, NB, None, 0, products), (0, NB, None, 1, relay_sums), (0, NB, None, 2, quarter_sums),
        (0, NB, None, 3, activate), (0, NB, None, 4, relay_acts), (0, NB, True, 5, far_acts),
        (0, NB, True, 6, input_grad_split), (0, NB - 1, False, 5, input_grad_whole),
    )

    @pl.loop(1, NB + 4)
    def _(t):
        for first, end, split, lag, stage in stages:
            b = t - lag
            runs = (b >= first) & (b < end)
            if split is not None:
                runs = runs & (in_split(b) if split else jnp.logical_not(in_split(b)))

            @pl.when(runs)
            def _(stage=stage, b=b):
                stage(b)

        @pl.when(t == 3)
        def _():
            put(xall.at[0, 1], xall.at[7, 0], s_move, xr.at[7, 0], z_up)
            put(xall.at[0, 1], xall.at[7, 1], s_move, xr.at[7, 1], z_down)

        @pl.when((t == 5) | (t == 7))
        def _():
            forward(7 - (t - 5) // 2)

        @pl.when(t == 9)
        def _():
            arrived(xall.at[5, 0], xr.at[5, 0])
            arrived(xall.at[5, 1], xr.at[5, 1])

        last = t - 6

        @pl.when((last >= 0) & (last < NB - 4) & (last % 4 == 3))
        def _():
            for i in range(4):
                sibling_done(last - i)
            weight_grads([blocks(xall, full, last - 3, 4), blocks(xsib, fsib, last - 3, 4)])

    sibling_done(NB - 4)
    sibling_done(NB - 3)
    weight_grads([blocks(xall, full, NB - 4, 2), blocks(xsib, fsib, NB - 4, 2)])
    sibling_done(NB - 2)
    weight_grads([blocks(xall, full, NB - 2, 1), blocks(xsib, fsib, NB - 2, 1)])
    acts_ready(NB - 1, full.at[NB - 1, far], rs.at[NB - 1, 4])
    sibling_done(NB - 1)
    weight_grads([blocks(xall, full, NB - 1, 1), blocks(xsib, fsib, NB - 1, 1)])

    def folded(values):
        rows = jnp.sum((values * values).reshape(-1, 8, values.shape[1]), axis=0)
        out = rows[:, 0:128]
        for i in range(1, values.shape[1] // 128):
            out += rows[:, 128 * i : 128 * (i + 1)]
        return out

    squares = jnp.zeros((8, 128), F32)
    stores = []
    for j in range(2):
        squares += folded(acc_in[j]) + folded(acc_out[j])
    sq[0] = squares

    for slot, where in group_two:
        put(sq.at[0], sqr1.at[slot], s_one, srs.at[0], where)
    for j in range(2):
        out_in[j] = acc_in[j].astype(BF16)
        out_out[j] = acc_out[j].astype(BF16)
        stores.append(pltpu.make_async_copy(out_in.at[j], o_gin.at[:, j * Q : (j + 1) * Q], ls.at[j]))
        stores.append(pltpu.make_async_copy(out_out.at[j], o_gout.at[j * Q : (j + 1) * Q], ls.at[2 + j]))
    for store in stores:
        store.start()
    input_grad(jnp.int32(NB - 1))
    arrived(sqr1.at[1:16], srs.at[0])
    whole = sq[0] + jnp.sum(sqr1[1:16], axis=0)
    sq[1] = whole
    for slot, where in group_one:
        put(sq.at[1], sqr2.at[slot], s_two, srs.at[1], where)

    arrived(dxr.at[1:11], srs.at[2])
    total = dxs[0].astype(F32)
    for i in range(1, 11):
        total += dxr[i].astype(F32)
    o_dx[...] = total.astype(BF16)

    arrived(sqr2.at[1:16], srs.at[1])
    o_sum[...] = whole + jnp.sum(sqr2[1:16], axis=0)

    for store in stores:
        store.wait()
    split = sum(1 for b in range(SPLIT) if b % EVERY < OF)
    left(got, s_sum)
    left(got.at[0 : 96 - 2 * split], s_act)
    left(got.at[0 : 62 + 2 * split], s_pass)
    left(got.at[0:60], s_move)
    left(got.at[0:48], s_core)
    left(part, s_half)
    left(sqr1.at[1:16], s_one)
    left(sqr2.at[1:16], s_two)


def scale_kernel(squares, dx, gin, gout, o_dx, o_gin, o_gout):
    total = jnp.sum(squares[...], keepdims=True)
    factor = 1.0 / jnp.sqrt(total / (2.0 * D * FW) + 1e-06)
    o_dx[...] = dx[...]
    o_gin[...] = (gin[...].astype(F32) * factor).astype(BF16)
    o_gout[...] = (gout[...].astype(F32) * factor).astype(BF16)


def scaled(squares, in_grad, grad_in, grad_out):
    steps = 2
    fixed = lambda shape: pl.BlockSpec(shape, lambda i: (0, 0))
    moving = lambda: pl.BlockSpec((W // steps, W), lambda i: (i, 0))
    return pl.pallas_call(
        scale_kernel,
        grid=(steps,),
        out_shape=(
            jax.ShapeDtypeStruct((ROWS, W), BF16),
            jax.ShapeDtypeStruct((W, W), BF16),
            jax.ShapeDtypeStruct((W, W), BF16),
        ),
        in_specs=[fixed((8, 128)), fixed((ROWS, W)), moving(), moving()],
        out_specs=(fixed((ROWS, W)), moving(), moving()),
    )(squares, in_grad, grad_in, grad_out)


def shards(tokens, w_in, w_out, out_grad):
    vmem = pl.BlockSpec(memory_space=pltpu.VMEM)
    hbm = pl.BlockSpec(memory_space=pl.ANY)
    dma = pltpu.SemaphoreType.DMA
    in_grad, grad_in, grad_out, squares = pl.pallas_call(
        kernel,
        out_shape=(
            jax.ShapeDtypeStruct((ROWS, W), BF16),
            jax.ShapeDtypeStruct((W, W), BF16),
            jax.ShapeDtypeStruct((W, W), BF16),
            jax.ShapeDtypeStruct((8, 128), F32),
        ),
        in_specs=[hbm] * 4,
        out_specs=(vmem, hbm, hbm, vmem),
        scratch_shapes=[
            pltpu.VMEM((NB // 2, 2, 2, ROWS, W), BF16),
            pltpu.VMEM((NB // 2, 2, 2, ROWS, W), BF16),
            pltpu.VMEM((2, W, W), BF16),
            pltpu.VMEM((2, W, W), BF16),
            pltpu.VMEM((NB, 4, 2, ROWS, Q), BF16),
            pltpu.VMEM((NB * 6, ROWS, Q), BF16),
            pltpu.VMEM((NB, 2, ROWS, Q), BF16),
            pltpu.VMEM((NB, 4, 2, 2, HALF, Q), BF16),
            pltpu.VMEM((NB, 2, 2, 2, HALF, Q), BF16),
            pltpu.VMEM((2, W, Q), F32),
            pltpu.VMEM((2, Q, W), F32),
            pltpu.VMEM((2, W, Q), BF16),
            pltpu.VMEM((2, Q, W), BF16),
            pltpu.VMEM((NB, ROWS, W), BF16),
            pltpu.VMEM((16, ROWS, W), BF16),
            pltpu.VMEM((2, 8, 128), F32),
            pltpu.VMEM((16, 8, 128), F32),
            pltpu.VMEM((16, 8, 128), F32),
            dma((4,)),
            dma((8,)),
            dma((NB // 2, 2)),
            dma((NB, 7)),
            dma((2,)),
            dma((3,)),
            dma((5,)),
        ],
        compiler_params=pltpu.CompilerParams(
            collective_id=0, has_side_effects=True, vmem_limit_bytes=60 * 2**20
        ),
        cost_estimate=pl.CostEstimate(
            flops=12_100_000_000, bytes_accessed=10_000_000, transcendentals=400_000
        ),
    )(tokens, w_in, w_out, out_grad)
    return scaled(squares, in_grad, grad_in, grad_out)


def solution(mesh):
    placed = (
        P(("gy", "gx"), "gz"),
        P("gz", ("gx", "gy")),
        P(("gx", "gy"), "gz"),
        P(("gy", "gx"), "gz"),
    )
    return jax.shard_map(
        shards,
        mesh=mesh,
        in_specs=placed,
        out_specs=(P(("gy", "gx"), "gz"), P("gz", ("gx", "gy")), P(("gx", "gy"), "gz")),
        check_vma=False,
    )
```

```python
import jax
import jax.numpy as jnp
from jax import lax
from jax.experimental import pallas as pl
from jax.experimental.pallas import tpu as pltpu
from jax.sharding import PartitionSpec as P

D = 6144
FW = 24576
GELU_C = 0.7978845608
MESH = pl.DeviceIdType.MESH

NB = 16
ROWS = 64
HALF = 32
W = 768
SPLIT, EVERY, OF = 14, 2, 1
Q = 384
F32 = jnp.float32
BF16 = jnp.bfloat16


def gelu_parts(values):
    square = values * values
    inner_arg = GELU_C * (values + 0.044715 * square * values)
    tanh_val = jnp.tanh(inner_arg)
    value_out = 0.5 * values * (1.0 + tanh_val)
    slope = 0.5 * (1.0 + tanh_val) + 0.5 * values * (1.0 - tanh_val * tanh_val) * GELU_C * (
        1.0 + 3.0 * 0.044715 * square
    )
    return (value_out, slope)


def contract(left, right, left_dim, right_dim):
    return lax.dot_general(
        left, right, (((left_dim,), (right_dim,)), ((), ())), preferred_element_type=F32
    )


def kernel(
    tok, win, wout, dy, o_dx, o_gin, o_gout, o_sum,
    xall, xsib, wown, wsib, part, got, xgot, full, fsib, acc_in, acc_out, out_in, out_out, dxs, dxr,
    sq, sqr1, sqr2,
    ls, ss, xr, rs, wrs, srs, crs,
):
    z, gy, gz = lax.axis_index("gx"), lax.axis_index("gy"), lax.axis_index("gz")
    yy, xh = gz // 2, gz % 2
    xl, core = gy // 2, gy % 2
    up, down, far = (yy + 1) % 4, (yy + 3) % 4, (yy + 2) % 4
    to_up, to_down = {"gz": up * 2 + xh}, {"gz": down * 2 + xh}
    hi_gz = yy * 2 + 1 - xh
    other_gy = (1 - xl) * 2 + core
    sib_gy = xl * 2 + 1 - core
    to_hi, to_lo, to_sib = {"gz": hi_gz}, {"gy": other_gy}, {"gy": sib_gy}
    z_up, z_down = {"gx": (z + 1) % 8}, {"gx": (z + 7) % 8}

    group_one = [
        (dz * 2 + k, {"gx": (z + dz) % 8, "gy": other_gy if k else gy})
        for dz in range(8) for k in range(2) if dz + k
    ]
    group_two = [
        (d * 4 + kx * 2 + kc, {
            "gz": ((yy + d) % 4) * 2 + (1 - xh if kx else xh),
            "gy": sib_gy if kc else gy,
        })
        for d in range(4) for kx in range(2) for kc in range(2) if d + kx + kc
    ]
    s_sum, s_act, s_pass, s_move, s_core, s_one, s_two, s_half = [ss.at[i] for i in range(8)]

    def put(src, dst, send, recv, where):
        pltpu.make_async_remote_copy(
            src_ref=src, dst_ref=dst, send_sem=send, recv_sem=recv,
            device_id=where, device_id_type=MESH,
        ).start()

    def arrived(ref, sem):
        pltpu.make_async_remote_copy(
            src_ref=ref, dst_ref=ref, send_sem=sem, recv_sem=sem,
            device_id=to_up, device_id_type=MESH,
        ).wait_recv()

    def left(ref, sem):
        pltpu.make_async_remote_copy(
            src_ref=ref, dst_ref=ref, send_sem=sem, recv_sem=sem,
            device_id=to_up, device_id_type=MESH,
        ).wait_send()

    loads = [
        pltpu.make_async_copy(tok, xall.at[0, 0, 0], ls.at[0]),
        pltpu.make_async_copy(dy, xall.at[0, 0, 1], ls.at[1]),
        pltpu.make_async_copy(win, wown.at[0], ls.at[2]),
        pltpu.make_async_copy(wout, wown.at[1], ls.at[3]),
    ]
    for load in loads:
        load.start()
    barrier = pltpu.get_barrier_semaphore()
    for _, where in group_one + group_two:
        pl.semaphore_signal(barrier, inc=1, device_id=where, device_id_type=MESH)
    acc_in[...] = jnp.zeros_like(acc_in)
    acc_out[...] = jnp.zeros_like(acc_out)
    loads[0].wait()
    loads[1].wait()
    pl.semaphore_wait(barrier, 30)

    put(xall.at[0, 0], xall.at[0, 1], s_move, xr.at[0, 1], to_lo)
    put(xall.at[0, 0], xall.at[1, 0], s_move, xr.at[1, 0], z_up)
    put(xall.at[0, 0], xall.at[1, 1], s_move, xr.at[1, 1], z_down)
    loads[2].wait()
    put(wown.at[0], wsib.at[0], s_core, wrs.at[0], to_sib)
    loads[3].wait()
    put(wown.at[1], wsib.at[1], s_core, wrs.at[1], to_sib)

    def one(b, x, g, which, w_in, w_out):
        h = contract(x, w_in, 1, 0).astype(BF16)
        part[b, 2 * which, 0] = h[:, :Q]
        part[b, 2 * which + 1, 0] = h[:, Q:]
        d = contract(g, w_out, 1, 1).astype(BF16)
        part[b, 2 * which, 1] = d[:, :Q]
        part[b, 2 * which + 1, 1] = d[:, Q:]

    def send_products(b):
        put(part.at[b, far, 0], got.at[6 * b], s_sum, rs.at[b, 0], to_up)
        put(part.at[b, far, 1], got.at[6 * b + 1], s_sum, rs.at[b, 0], to_down)
        put(part.at[b, up, 1], got.at[6 * b + 2], s_sum, rs.at[b, 1], to_up)
        put(part.at[b, down, 0], got.at[6 * b + 3], s_sum, rs.at[b, 1], to_down)

    one(0, xall[0, 0, 0], xall[0, 0, 1], 0, wown[0], wown[1])
    arrived(wsib.at[0], wrs.at[0])
    h = contract(xall[0, 0, 0], wsib[0], 1, 0).astype(BF16)
    part[0, 2, 0], part[0, 3, 0] = h[:, :Q], h[:, Q:]
    arrived(wsib.at[1], wrs.at[1])
    d = contract(xall[0, 0, 1], wsib[1], 1, 1).astype(BF16)
    part[0, 2, 1], part[0, 3, 1] = d[:, :Q], d[:, Q:]
    send_products(0)
    put(xall.at[0, 0], xsib.at[0, 0], s_half, rs.at[0, 6], to_sib)

    def products(b):
        slot, side = b // 2, b % 2

        @pl.when(b < 10)
        def _():
            arrived(xall.at[slot, side], xr.at[slot, side])

        @pl.when((b > 1) & (b < 8) & (side == 0))
        def _():
            put(xall.at[slot, 0], xall.at[slot + 1, 0], s_move, xr.at[slot + 1, 0], z_up)

        @pl.when((b > 1) & (b < 6) & (side == 1))
        def _():
            put(xall.at[slot, 1], xall.at[slot + 1, 1], s_move, xr.at[slot + 1, 1], z_down)

        @pl.when(b == 8)
        def _():
            put(xall.at[4, 0], xall.at[4, 1], s_move, xr.at[4, 1], to_lo)

        for k, w in enumerate((wown, wsib)):
            one(b, xall[slot, side, 0], xall[slot, side, 1], k, w[0], w[1])
        send_products(b)
        put(xall.at[slot, side], xsib.at[slot, side], s_half, rs.at[b, 6], to_sib)

    def forward(s):
        arrived(xall.at[s, 0], xr.at[s, 0])
        put(xall.at[s, 0], xall.at[s - 1, 0], s_move, xr.at[s - 1, 0], z_up)
        arrived(xall.at[s, 1], xr.at[s, 1])
        put(xall.at[s, 1], xall.at[s - 1, 1], s_move, xr.at[s - 1, 1], z_down)

    def relay_sums(b):
        arrived(got.at[pl.ds(6 * b, 2)], rs.at[b, 0])
        part[b, up, 0] = (part[b, up, 0].astype(F32) + got[6 * b].astype(F32)).astype(BF16)
        put(part.at[b, up, 0], got.at[6 * b + 4], s_sum, rs.at[b, 1], to_up)
        part[b, down, 1] = (
            part[b, down, 1].astype(F32) + got[6 * b + 1].astype(F32)
        ).astype(BF16)
        put(part.at[b, down, 1], got.at[6 * b + 5], s_sum, rs.at[b, 1], to_down)

    def quarter_sums(b):
        arrived(got.at[pl.ds(6 * b + 2, 4)], rs.at[b, 1])
        part[b, yy, 0] = (
            part[b, yy, 0].astype(F32) + got[6 * b + 3].astype(F32) + got[6 * b + 4].astype(F32)
        ).astype(BF16)
        part[b, yy, 1] = (
            part[b, yy, 1].astype(F32) + got[6 * b + 2].astype(F32) + got[6 * b + 5].astype(F32)
        ).astype(BF16)
        put(part.at[b, yy], xgot.at[b], s_act, rs.at[b, 2], to_hi)

    def in_split(b):
        return (b < SPLIT) & (b % EVERY < OF)

    def activate(b):
        arrived(xgot.at[b], rs.at[b, 2])
        value_out, slope = gelu_parts(part[b, yy, 0].astype(F32) + xgot[b, 0].astype(F32))
        d_pre = (part[b, yy, 1].astype(F32) + xgot[b, 1].astype(F32)) * slope
        full[b, yy, :, 0] = value_out.astype(BF16).reshape(2, HALF, Q)
        full[b, yy, :, 1] = d_pre.astype(BF16).reshape(2, HALF, Q)

        @pl.when(in_split(b))
        def _():
            mine = full.at[b, yy, xh]
            put(mine, mine, s_act, rs.at[b, 3], to_up)
            put(mine, mine, s_act, rs.at[b, 3], to_down)

        @pl.when(jnp.logical_not(in_split(b)))
        def _():
            mine = full.at[b, yy]
            put(mine, mine, s_act, rs.at[b, 3], to_up)
            put(mine, mine, s_act, rs.at[b, 3], to_down)

    def relay_acts(b):
        @pl.when(in_split(b))
        def _():
            arrived(full.at[b, 0], rs.at[b, 3])
            low, high = full.at[b, down, xh], full.at[b, up, xh]
            put(low.at[0], low.at[0], s_pass, rs.at[b, 4], to_up)
            put(high.at[1], high.at[1], s_pass, rs.at[b, 4], to_down)
            put(low, low, s_pass, rs.at[b, 5], to_hi)
            put(high, high, s_pass, rs.at[b, 5], to_hi)

        @pl.when(jnp.logical_not(in_split(b)))
        def _():
            arrived(full.at[b, 0:2], rs.at[b, 3])
            low, high = full.at[b, down, :, 0], full.at[b, up, :, 1]
            put(low, low, s_pass, rs.at[b, 4], to_up)
            put(high, high, s_pass, rs.at[b, 4], to_down)

    def far_acts(b):
        mine = full.at[b, far, xh]
        arrived(mine, rs.at[b, 4])
        put(mine, mine, s_pass, rs.at[b, 5], to_hi)

    def acts_ready(b, ready, sem):
        arrived(ready, sem)
        put(full.at[b, 2:4], fsib.at[b], s_half, rs.at[b, 6], to_sib)

    def input_grad(b):
        own, sib = [
            jnp.concatenate([full[b, q, :, 1].reshape(ROWS, Q) for q in qs], axis=1)
            for qs in ((0, 1), (2, 3))
        ]
        partial = contract(own, wown[0], 1, 1) + contract(sib, wsib[0], 1, 1)

        slot, side = b // 2, b % 2

        @pl.when(b < 8)
        def _():
            dxs[b] = partial.astype(BF16)

            @pl.when((b > 1) & (side == 0))
            def _():
                put(dxs.at[b], dxr.at[b], s_pass, srs.at[2], {"gx": (z + 8 - slot) % 8})

            @pl.when((b > 1) & (side == 1))
            def _():
                put(dxs.at[b], dxr.at[b], s_pass, srs.at[2], {"gx": (z + slot) % 8})

            @pl.when(b == 1)
            def _():
                put(dxs.at[1], dxr.at[1], s_pass, srs.at[2], to_lo)

        @pl.when(b == 8)
        def _():
            dxs[b] = partial.astype(BF16)
            put(dxs.at[8], dxr.at[8], s_pass, srs.at[2], {"gx": (z + 4) % 8})

        @pl.when((b == 9) | (b == 10))
        def _():
            dxs[b] = partial.astype(BF16)

        @pl.when(b > 10)
        def _():
            arrived(dxr.at[b], crs.at[b - 11])
            dxs[b] = (partial + dxr[b].astype(F32)).astype(BF16)

        @pl.when((b > 8) & (b < NB - 2) & (side == 0))
        def _():
            put(dxs.at[b], dxr.at[b + 2], s_pass, crs.at[b - 9], z_down)

        @pl.when((b > 8) & (b < NB - 2) & (side == 1))
        def _():
            put(dxs.at[b], dxr.at[b + 2], s_pass, crs.at[b - 9], z_up)

        @pl.when(b == NB - 2)
        def _():
            put(dxs.at[b], dxr.at[9], s_pass, srs.at[2], {"gx": (z + 7) % 8, "gy": other_gy})

        @pl.when(b == NB - 1)
        def _():
            put(dxs.at[b], dxr.at[10], s_pass, srs.at[2], {"gx": (z + 1) % 8, "gy": other_gy})

    def input_grad_split(b):
        acts_ready(b, full.at[b, 0:3, 0], rs.at[b, 5])
        input_grad(b)

    def input_grad_whole(b):
        acts_ready(b, full.at[b, far], rs.at[b, 4])
        input_grad(b)

    def blocks(tokens, acts, first, count):
        if count > 1:
            slots = pl.ds(first // 2, count // 2)
            x = tokens[slots, :, 0].reshape(count * ROWS, W)
            g = tokens[slots, :, 1].reshape(count * ROWS, W)
        else:
            x, g = tokens[first // 2, first % 2, 0], tokens[first // 2, first % 2, 1]
        act = [acts[pl.ds(first, count), q, :, 0].reshape(count * ROWS, Q) for q in range(2)]
        d_pre = [acts[pl.ds(first, count), q, :, 1].reshape(count * ROWS, Q) for q in range(2)]
        return x, g, act, d_pre

    def weight_grads(parts):
        x_t = jnp.concatenate([part[0] for part in parts], axis=0).T
        g = jnp.concatenate([part[1] for part in parts], axis=0)
        for q in range(2):
            act_t = jnp.concatenate([part[2][q] for part in parts], axis=0).T
            d_pre = jnp.concatenate([part[3][q] for part in parts], axis=0)
            acc_in[q] += contract(x_t, d_pre, 1, 0)
            acc_out[q] += contract(act_t, g, 1, 0)

    def sibling_done(b):
        arrived(got.at[0:8], rs.at[b, 6])

    stages = (
        (1, NB, None, 0, products), (0, NB, None, 1, relay_sums), (0, NB, None, 2, quarter_sums),
        (0, NB, None, 3, activate), (0, NB, None, 4, relay_acts), (0, NB, True, 5, far_acts),
        (0, NB, True, 6, input_grad_split), (0, NB - 1, False, 5, input_grad_whole),
    )

    @pl.loop(1, NB + 4)
    def _(t):
        for first, end, split, lag, stage in stages:
            b = t - lag
            runs = (b >= first) & (b < end)
            if split is not None:
                runs = runs & (in_split(b) if split else jnp.logical_not(in_split(b)))

            @pl.when(runs)
            def _(stage=stage, b=b):
                stage(b)

        @pl.when(t == 3)
        def _():
            put(xall.at[0, 1], xall.at[7, 0], s_move, xr.at[7, 0], z_up)
            put(xall.at[0, 1], xall.at[7, 1], s_move, xr.at[7, 1], z_down)

        @pl.when((t == 5) | (t == 7))
        def _():
            forward(7 - (t - 5) // 2)

        @pl.when(t == 9)
        def _():
            arrived(xall.at[5, 0], xr.at[5, 0])
            arrived(xall.at[5, 1], xr.at[5, 1])

        last = t - 6

        @pl.when((last >= 0) & (last < NB - 4) & (last % 4 == 3))
        def _():
            for i in range(4):
                sibling_done(last - i)
            weight_grads([blocks(xall, full, last - 3, 4), blocks(xsib, fsib, last - 3, 4)])

    sibling_done(NB - 4)
    sibling_done(NB - 3)
    weight_grads([blocks(xall, full, NB - 4, 2), blocks(xsib, fsib, NB - 4, 2)])
    sibling_done(NB - 2)
    weight_grads([blocks(xall, full, NB - 2, 1), blocks(xsib, fsib, NB - 2, 1)])
    acts_ready(NB - 1, full.at[NB - 1, far], rs.at[NB - 1, 4])
    sibling_done(NB - 1)
    weight_grads([blocks(xall, full, NB - 1, 1), blocks(xsib, fsib, NB - 1, 1)])

    def folded(values):
        rows = jnp.sum((values * values).reshape(-1, 8, values.shape[1]), axis=0)
        out = rows[:, 0:128]
        for i in range(1, values.shape[1] // 128):
            out += rows[:, 128 * i : 128 * (i + 1)]
        return out

    squares = jnp.zeros((8, 128), F32)
    stores = []
    for j in range(2):
        squares += folded(acc_in[j]) + folded(acc_out[j])
    sq[0] = squares

    for slot, where in group_two:
        put(sq.at[0], sqr1.at[slot], s_one, srs.at[0], where)
    for j in range(2):
        out_in[j] = acc_in[j].astype(BF16)
        out_out[j] = acc_out[j].astype(BF16)
        stores.append(pltpu.make_async_copy(out_in.at[j], o_gin.at[:, j * Q : (j + 1) * Q], ls.at[j]))
        stores.append(pltpu.make_async_copy(out_out.at[j], o_gout.at[j * Q : (j + 1) * Q], ls.at[2 + j]))
    for store in stores:
        store.start()
    input_grad(jnp.int32(NB - 1))
    arrived(sqr1.at[1:16], srs.at[0])
    whole = sq[0] + jnp.sum(sqr1[1:16], axis=0)
    sq[1] = whole
    for slot, where in group_one:
        put(sq.at[1], sqr2.at[slot], s_two, srs.at[1], where)

    arrived(dxr.at[1:11], srs.at[2])
    total = dxs[0].astype(F32)
    for i in range(1, 11):
        total += dxr[i].astype(F32)
    o_dx[...] = total.astype(BF16)

    arrived(sqr2.at[1:16], srs.at[1])
    o_sum[...] = whole + jnp.sum(sqr2[1:16], axis=0)

    for store in stores:
        store.wait()
    split = sum(1 for b in range(SPLIT) if b % EVERY < OF)
    left(got, s_sum)
    left(got.at[0 : 96 - 2 * split], s_act)
    left(got.at[0 : 62 + 2 * split], s_pass)
    left(got.at[0:60], s_move)
    left(got.at[0:48], s_core)
    left(part, s_half)
    left(sqr1.at[1:16], s_one)
    left(sqr2.at[1:16], s_two)


def scale_kernel(squares, dx, gin, gout, o_dx, o_gin, o_gout):
    total = jnp.sum(squares[...], keepdims=True)
    factor = 1.0 / jnp.sqrt(total / (2.0 * D * FW) + 1e-06)
    o_dx[...] = dx[...]
    o_gin[...] = (gin[...].astype(F32) * factor).astype(BF16)
    o_gout[...] = (gout[...].astype(F32) * factor).astype(BF16)


def scaled(squares, in_grad, grad_in, grad_out):
    steps = 2
    fixed = lambda shape: pl.BlockSpec(shape, lambda i: (0, 0))
    moving = lambda: pl.BlockSpec((W // steps, W), lambda i: (i, 0))
    return pl.pallas_call(
        scale_kernel,
        grid=(steps,),
        out_shape=(
            jax.ShapeDtypeStruct((ROWS, W), BF16),
            jax.ShapeDtypeStruct((W, W), BF16),
            jax.ShapeDtypeStruct((W, W), BF16),
        ),
        in_specs=[fixed((8, 128)), fixed((ROWS, W)), moving(), moving()],
        out_specs=(fixed((ROWS, W)), moving(), moving()),
    )(squares, in_grad, grad_in, grad_out)


def shards(tokens, w_in, w_out, out_grad):
    vmem = pl.BlockSpec(memory_space=pltpu.VMEM)
    hbm = pl.BlockSpec(memory_space=pl.ANY)
    dma = pltpu.SemaphoreType.DMA
    in_grad, grad_in, grad_out, squares = pl.pallas_call(
        kernel,
        out_shape=(
            jax.ShapeDtypeStruct((ROWS, W), BF16),
            jax.ShapeDtypeStruct((W, W), BF16),
            jax.ShapeDtypeStruct((W, W), BF16),
            jax.ShapeDtypeStruct((8, 128), F32),
        ),
        in_specs=[hbm] * 4,
        out_specs=(vmem, hbm, hbm, vmem),
        scratch_shapes=[
            pltpu.VMEM((NB // 2, 2, 2, ROWS, W), BF16),
            pltpu.VMEM((NB // 2, 2, 2, ROWS, W), BF16),
            pltpu.VMEM((2, W, W), BF16),
            pltpu.VMEM((2, W, W), BF16),
            pltpu.VMEM((NB, 4, 2, ROWS, Q), BF16),
            pltpu.VMEM((NB * 6, ROWS, Q), BF16),
            pltpu.VMEM((NB, 2, ROWS, Q), BF16),
            pltpu.VMEM((NB, 4, 2, 2, HALF, Q), BF16),
            pltpu.VMEM((NB, 2, 2, 2, HALF, Q), BF16),
            pltpu.VMEM((2, W, Q), F32),
            pltpu.VMEM((2, Q, W), F32),
            pltpu.VMEM((2, W, Q), BF16),
            pltpu.VMEM((2, Q, W), BF16),
            pltpu.VMEM((NB, ROWS, W), BF16),
            pltpu.VMEM((16, ROWS, W), BF16),
            pltpu.VMEM((2, 8, 128), F32),
            pltpu.VMEM((16, 8, 128), F32),
            pltpu.VMEM((16, 8, 128), F32),
            dma((4,)),
            dma((8,)),
            dma((NB // 2, 2)),
            dma((NB, 7)),
            dma((2,)),
            dma((3,)),
            dma((5,)),
        ],
        compiler_params=pltpu.CompilerParams(
            collective_id=0, has_side_effects=True, vmem_limit_bytes=60 * 2**20
        ),
        cost_estimate=pl.CostEstimate(
            flops=12_100_000_000, bytes_accessed=10_000_000, transcendentals=400_000
        ),
    )(tokens, w_in, w_out, out_grad)
    return scaled(squares, in_grad, grad_in, grad_out)


def solution(mesh):
    placed = (
        P(("gy", "gx"), "gz"),
        P("gz", ("gx", "gy")),
        P(("gx", "gy"), "gz"),
        P(("gy", "gx"), "gz"),
    )
    return jax.shard_map(
        shards,
        mesh=mesh,
        in_specs=placed,
        out_specs=(P(("gy", "gx"), "gz"), P("gz", ("gx", "gy")), P(("gx", "gy"), "gz")),
        check_vma=False,
    )
```
